512 devices in a mesh: ctx: 64 (over z_lo, y, core), exp: 8 (over x, z_hi).
Axes of the slice: x: 4, y: 4, z: 16 (z_hi: 2, z_lo: 8; z = z_hi * 8 + z_lo), core: 2. Of those that a mesh axis runs over, the one named last changes fastest.
Arguments:
- queries: bfloat16 [8192, 36864], P('ctx', 'exp'), may hold values from -40 to 40
- latents: bfloat16 [8192, 576], P('ctx'), may hold values from -8 to 8
- out_grad: bfloat16 [8192, 32768], P('ctx', 'exp'), may hold values from -6 to 6
- block_start: int32 [64], P('ctx'), may hold values from 0 to 63, as said below
- moe_grad: bfloat16 [8192, 3584], P(('ctx', 'exp')), may hold values from -6 to 6
- affinity: float32 [8192, 8], P(('ctx', 'exp')), may hold values from 0.05 to 0.95
- expert_ids: int32 [8192, 8], P(('ctx', 'exp')), may hold values from 0 to 255, as said below
- expert_out: bfloat16 [64, 8, 8, 20, 3584], P('ctx', 'exp'), may hold values from -0.09375 to 0.09375
Outputs:
- query_grad: bfloat16 [8192, 36864], P('ctx', 'exp')
- latent_grad: bfloat16 [8192, 576], P('ctx')
- logit_grad: float32 [8192, 8], P(('ctx', 'exp'))
The draws below stay inside these ranges and needn't reach their ends.
Inputs may be any that keep to these rules, and one draw needn't show every extreme that they name: block_start[b] lies between max(0, b - 32) and b, and equals b - 32 for some block b. `expert_ids`: each token names 8 different experts, lying in at most four groups; expert x belongs to group x // 32. Of the 128 copies of one device's tokens, at most 20 name experts of any one group, and for every ctx index some group receives exactly 20 copies from each of the 8 devices of that ctx index.
All inputs are finite; a program needn't handle non-finite values.
Results may differ from the reference program's by a relative error of at most 0.0095.
Values may be sent and summed in bfloat16 or wider, within the bound.
No kernel may reach another device: no remote copies, remote signals or barrier semaphores. Data moves between devices by JAX's collectives and lax.ppermute only.
A program may use at most 128 MiB of HBM per device.

```python
import jax
import jax.numpy as jnp
from jax import lax

HEADS = 64
LAT = 512
ROPE = 64
D = 3584
TOP = 8
TOK_DEV = 128
TOKENS = 8192
HALF = 32
MTOK = 16
MEAN = 16
CAP = 20
EXP_GROUP = 32
N_CTX = 64
N_EXP = 8


def latent_rows(key):
    noise_base = jax.random.normal(key, (TOKENS, LAT + ROPE), jnp.float32)
    return noise_base


def draw_latents(key, part):
    return latent_rows(key).astype(jnp.bfloat16)


def draw_queries(key, part):
    key = jax.random.fold_in(key, 3)
    own_part = 0.6 * jax.random.normal(key, (TOKENS, HEADS, LAT + ROPE), jnp.float32)
    return own_part.reshape(TOKENS, HEADS * (LAT + ROPE)).astype(jnp.bfloat16)


def draw_block_start(key, part):
    key = jax.random.fold_in(key, 11)
    factors = jax.random.randint(jax.random.fold_in(key, 1), (3, N_CTX), 0, HALF + 1)
    reach_len = factors[0] * factors[1] * factors[2] // (HALF * HALF)
    blocks = jnp.arange(N_CTX, dtype=jnp.int32)
    chosen = jax.random.randint(jax.random.fold_in(key, 2), (), HALF, N_CTX)
    reach_len = jnp.where(blocks == chosen, HALF, reach_len)
    return jnp.maximum(blocks - reach_len, 0).astype(jnp.int32)


def draw_expert_ids(key, part):
    key = jax.random.fold_in(key, 23)
    device_count = N_CTX * N_EXP
    pair_count = MTOK * TOP // 2
    pair_mean = MEAN // 2
    pair_extra = (CAP - MEAN) // 2
    favored = jnp.repeat(jax.random.randint(jax.random.fold_in(key, 1), (N_CTX,), 0, N_EXP), N_EXP)
    rotation = jax.random.randint(jax.random.fold_in(key, 2), (device_count,), 0, N_EXP - 1)
    unit_ids = jnp.arange(pair_extra, dtype=jnp.int32)
    target = (favored[:, None] + 1 + (rotation[:, None] + unit_ids[None, :]) % (N_EXP - 1)) % N_EXP
    groups = jnp.arange(N_EXP, dtype=jnp.int32)
    removed = jnp.sum((target[:, :, None] == groups[None, None, :]).astype(jnp.int32), axis=1)
    owner_load = pair_mean - removed + pair_extra * (favored[:, None] == groups[None, :]).astype(jnp.int32)
    upper_edges = jnp.cumsum(owner_load, axis=1)
    pair_ids = jnp.arange(pair_count, dtype=jnp.int32)
    pair_owner = jnp.sum((pair_ids[None, :, None] >= upper_edges[:, None, :]).astype(jnp.int32), axis=2)
    perm_keys = jax.random.split(jax.random.fold_in(key, 3), device_count)
    token_order = jax.vmap(lambda single: jax.random.permutation(single, MTOK))(perm_keys)
    token_id = token_order[:, pair_ids % MTOK]
    pair_rank = jnp.broadcast_to(pair_ids // MTOK, (device_count, pair_count))
    offset_draw = jax.random.randint(jax.random.fold_in(key, 4), (device_count, 1), 0, EXP_GROUP)
    dev_rows = jnp.broadcast_to(jnp.arange(device_count, dtype=jnp.int32)[:, None], (device_count, pair_count))
    id_table = jnp.zeros((device_count, MTOK, TOP), jnp.int32)
    for within in range(2):
        gate_rank = 2 * pair_rank + within
        chosen_ids = pair_owner * EXP_GROUP + (gate_rank + offset_draw) % EXP_GROUP
        id_table = id_table.at[dev_rows, token_id, gate_rank].set(chosen_ids)
    return id_table.reshape(TOKENS, TOP).astype(jnp.int32)


def steps_of(key, extent, shards, smallest, largest):
    factor_of, own = 1.0, jax.random.fold_in(key, 6)
    for dim, shards_of in shards:
        steps = jnp.exp(jax.random.uniform(jax.random.fold_in(own, dim), (shards_of,), jnp.float32, smallest / len(shards), largest / len(shards)))
        factor_of = factor_of * jnp.repeat(steps, extent[dim] // shards_of).reshape([-1 if axis == dim else 1 for axis in range(len(extent))])
    return factor_of


def scatter_about(rng, extent, deviation, limit, shards=(), kind=jnp.bfloat16):
    values = jax.random.normal(rng, extent, jnp.float32) * deviation
    if len(shards) > 0:
        values = steps_of(rng, extent, shards, -0.22, 0.18) * values
    return jnp.clip(values, min=-limit, max=limit).astype(kind)


def setup_inputs(seed: int = 0) -> dict:
    key_list = jax.random.split(jax.random.key(seed), 9)
    return {
        "queries": draw_queries(jax.random.fold_in(key_list[8], 71), 0),
        "latents": draw_latents(jax.random.fold_in(key_list[8], 71), 0),
        "out_grad": scatter_about(key_list[2], (TOKENS, HEADS * LAT), 1.0, 6.0, ((0, 64), (1, 8))),
        "block_start": draw_block_start(jax.random.fold_in(key_list[8], 71), 0),
        "moe_grad": scatter_about(key_list[4], (TOKENS, D), 1.0, 6.0, ((0, 512),)),
        "affinity": jnp.clip(0.05 + 0.9 * jax.random.uniform(key_list[5], (TOKENS, TOP), jnp.float32) ** steps_of(key_list[5], (TOKENS, TOP), ((0, 512),), -0.2, 0.2), 0.05, 0.95),
        "expert_ids": draw_expert_ids(jax.random.fold_in(key_list[8], 71), 0),
        "expert_out": scatter_about(key_list[7], (N_CTX, N_EXP, N_EXP, CAP, D), D ** -0.5, 0.09375, ((0, 64), (1, 8))),
    }


SCALE = 192.0 ** -0.5
ROUTE_SCALE = 2.5


def block_scores(query_block, key_rows, distance, causal):
    scores = SCALE * jnp.einsum("ihc,jc->hij", query_block.astype(jnp.float32), key_rows.astype(jnp.float32))
    allowed = jnp.logical_or(distance > 0, causal)
    return jnp.where(allowed[None], scores, -jnp.inf)


def attention_grads(queries, latents, out_grad, block_start):
    kv_width = LAT + ROPE
    query_all = queries.reshape(TOKENS, HEADS, kv_width)
    grad_all = out_grad.reshape(TOKENS, HEADS, LAT)
    position = jnp.arange(TOK_DEV, dtype=jnp.int32)
    causal = position[:, None] >= position[None, :]

    def one_block(latent_acc, block_id):
        row_start = (block_id * TOK_DEV).astype(jnp.int32)
        query_block = lax.dynamic_slice_in_dim(query_all, row_start, TOK_DEV, 0)
        grad_block = lax.dynamic_slice_in_dim(grad_all, row_start, TOK_DEV, 0)
        reach_len = block_id - block_start[block_id]

        def keys_at(distance):
            return lax.dynamic_slice_in_dim(latents, ((block_id - distance) * TOK_DEV).astype(jnp.int32), TOK_DEV, 0)

        def stats_step(distance, state_pair):
            running_max, running_sum = state_pair
            scores = block_scores(query_block, keys_at(distance), distance, causal)
            new_max = jnp.maximum(running_max, jnp.max(scores, axis=2))
            running_sum = running_sum * jnp.exp(running_max - new_max) + jnp.sum(jnp.exp(scores - new_max[:, :, None]), axis=2)
            return new_max, running_sum

        initial = (jnp.full((HEADS, TOK_DEV), -jnp.inf, jnp.float32), jnp.zeros((HEADS, TOK_DEV), jnp.float32))
        running_max, running_sum = lax.fori_loop(0, reach_len + 1, stats_step, initial)
        log_total = running_max + jnp.log(running_sum)

        def probs_at(distance):
            key_rows = keys_at(distance)
            scores = block_scores(query_block, key_rows, distance, causal)
            return key_rows, jnp.exp(scores - log_total[:, :, None])

        def out_step(distance, attn_out):
            key_rows, prob_rows = probs_at(distance)
            probs_low = prob_rows.astype(jnp.bfloat16)
            return attn_out + jnp.einsum("hij,jc->hic", probs_low.astype(jnp.float32), key_rows[:, :LAT].astype(jnp.float32))

        attn_out = lax.fori_loop(0, reach_len + 1, out_step, jnp.zeros((HEADS, TOK_DEV, LAT), jnp.float32))
        row_delta = jnp.einsum("ihc,hic->hi", grad_block.astype(jnp.float32), attn_out)

        def grad_step(distance, state_pair):
            query_acc, latent_sum = state_pair
            key_rows, prob_rows = probs_at(distance)
            probs_low = prob_rows.astype(jnp.bfloat16)
            prob_grad = jnp.einsum("ihc,jc->hij", grad_block.astype(jnp.float32), key_rows[:, :LAT].astype(jnp.float32))
            score_low = (prob_rows * (prob_grad - row_delta[:, :, None])).astype(jnp.bfloat16)
            query_acc = query_acc + SCALE * jnp.einsum("hij,jc->ihc", score_low.astype(jnp.float32), key_rows.astype(jnp.float32))
            key_term = SCALE * jnp.einsum("hij,ihc->jc", score_low.astype(jnp.float32), query_block.astype(jnp.float32))
            value_term = jnp.einsum("hij,ihc->jc", probs_low.astype(jnp.float32), grad_block.astype(jnp.float32))
            grad_term = key_term + jnp.pad(value_term, ((0, 0), (0, ROPE)))
            key_start = ((block_id - distance) * TOK_DEV).astype(jnp.int32)
            current = lax.dynamic_slice_in_dim(latent_sum, key_start, TOK_DEV, 0)
            latent_sum = lax.dynamic_update_slice_in_dim(latent_sum, current + grad_term, key_start, 0)
            return query_acc, latent_sum

        query_acc, latent_acc = lax.fori_loop(0, reach_len + 1, grad_step, (jnp.zeros((TOK_DEV, HEADS, kv_width), jnp.float32), latent_acc))
        return latent_acc, query_acc.astype(jnp.bfloat16)

    latent_acc, query_blocks = lax.scan(one_block, jnp.zeros((TOKENS, kv_width), jnp.float32), jnp.arange(N_CTX, dtype=jnp.int32))
    return query_blocks.reshape(TOKENS, HEADS * kv_width), latent_acc.astype(jnp.bfloat16)


def routing_grads(moe_grad, affinity, expert_ids, expert_out):
    device_count = N_CTX * N_EXP
    copies = MTOK * TOP
    owner_id = (expert_ids // EXP_GROUP).reshape(device_count, copies)
    copy_order = jnp.arange(copies, dtype=jnp.int32)
    earlier = copy_order[:, None] > copy_order[None, :]
    slot_index = jnp.sum(jnp.logical_and(owner_id[:, :, None] == owner_id[:, None, :], earlier[None]).astype(jnp.int32), axis=2)
    saved_all = expert_out.reshape(N_CTX * N_EXP * N_EXP * CAP, D)
    grad_rows = moe_grad.reshape(device_count, MTOK, D)

    def one_device(inputs):
        device, owner_row, slot_row, grad_block = inputs
        ctx_index = device // N_EXP
        exp_index = device % N_EXP
        flat_index = (((ctx_index * N_EXP + owner_row) * N_EXP + exp_index) * CAP + slot_row).astype(jnp.int32)
        saved_rows = jnp.take(saved_all, flat_index, axis=0)
        repeated = jnp.repeat(grad_block, TOP, axis=0)
        return jnp.einsum("fd,fd->f", saved_rows.astype(jnp.float32), repeated.astype(jnp.float32))

    gate_grad = lax.map(one_device, (jnp.arange(device_count, dtype=jnp.int32), owner_id, slot_index, grad_rows)).reshape(TOKENS, TOP)
    aff_total = jnp.sum(affinity, axis=1, keepdims=True)
    weighted = jnp.sum(gate_grad * affinity, axis=1, keepdims=True) / aff_total
    return (ROUTE_SCALE / aff_total) * (gate_grad - weighted) * affinity * (1.0 - affinity)


def reference(queries, latents, out_grad, block_start, moe_grad, affinity, expert_ids, expert_out):
    query_grad, latent_grad = attention_grads(queries, latents, out_grad, block_start)
    logit_grad = routing_grads(moe_grad, affinity, expert_ids, expert_out)
    return (query_grad, latent_grad, logit_grad)
```

```python
import jax
import jax.numpy as jnp
from jax import lax
from jax.experimental import pallas as pl
from jax.experimental.pallas import tpu as pltpu
from jax.sharding import Mesh, PartitionSpec as P

SCALE = 192.0 ** (-0.5)
EXP2_SCALE = SCALE * 1.4426950408889634
NEG = -1e30
BLK = 128
TILE = 2 * BLK
CHUNK = 256
ROWS = 8 * BLK
NT = (((1,), (1,)), ((), ()))
TN = (((0,), (0,)), ((), ()))


def each_copy(info, far, near, sem, tile, outward):
    copies = []
    for half in range(2):
        block = 2 * tile + half
        plane, turn = block // 4, (block + 4 - info[4]) % 4
        for part, pieces in enumerate(far):
            there = pieces.at[turn, :, plane] if part == 0 else pieces.at[:, turn, plane]
            here = near.at[half, part]
            pair = (here, there) if outward else (there, here)
            copies.append(pltpu.make_async_copy(*pair, sem.at[half, part]))
    return copies


def tile_span(info):
    own = info[3]
    last = own // 2
    first = jnp.minimum(jnp.minimum(info[0], info[1]) // 2, last)
    return first, last


def row_limits(info, group):
    return (info[0], info[3]) if group == 0 else (info[1], info[2])


def block_bias(info, group, tile):
    low, high = row_limits(info, group)
    return [jnp.where(jnp.logical_and(2 * tile + half >= low, 2 * tile + half <= high), 0.0, NEG)
            for half in range(2)]


def tile_used(info, group, tile):
    low, high = row_limits(info, group)
    return jnp.logical_and(2 * tile + 1 >= low, jnp.logical_and(2 * tile <= high, low <= high))


def masked(info, s, group, tile, diagonal, parts):
    bias = block_bias(info, group, tile)
    halves = []
    for half in range(2):
        part = s[half * BLK:(half + 1) * BLK] + bias[half]
        if diagonal:
            place = lax.broadcasted_iota(jnp.int32, part.shape, 0)
            row = lax.broadcasted_iota(jnp.int32, part.shape, 1) % BLK
            size = BLK // parts // 4
            key = ((place // size + info[5]) % 4) * (BLK // 4) + (place // (4 * size)) * size + place % size
            later = jnp.logical_and(key > row, info[3] == 2 * tile + half)
            part = jnp.where(later, NEG, part)
        halves.append(part)
    return halves[0], halves[1]


def load_keys(info, kv, keys, sem):
    first, last = tile_span(info)

    def begin(tile, _):
        for copy in each_copy(info, kv, keys.at[tile], sem.at[tile], tile, False):
            copy.start()
        return 0

    lax.fori_loop(first, last + 1, begin, 0)


def wait_keys(info, kv, keys, sem, tile):
    for copy in each_copy(info, kv, keys.at[tile], sem.at[tile], tile, False):
        copy.wait()


def split_heads(rows, heads):
    width = heads.shape[1]
    for pair in range(ROWS // BLK // 2):
        both = rows[:, 2 * width * pair:2 * width * (pair + 1)]
        heads[pl.ds(2 * pair * BLK, BLK), :] = both[:, :width]
        heads[pl.ds((2 * pair + 1) * BLK, BLK), :] = both[:, width:]


def join_heads(heads, rows):
    width = heads.shape[1]
    for pair in range(ROWS // BLK // 2):
        both = [heads[pl.ds((2 * pair + i) * BLK, BLK), :] * SCALE for i in range(2)]
        rows[:, 2 * width * pair:2 * width * (pair + 1)] = jnp.concatenate(both, axis=1).astype(rows.dtype)


def stats_kernel(parts, info, q_own, q_sib, g_own, g_sib, *refs):
    kv = refs[:parts]
    out, qs, gs, keys, m_ref, l_ref, d_ref, sem = refs[parts:]
    width, lat = qs.shape[2], gs.shape[2]
    load_keys(info, kv, keys, sem)
    for group, (q, g) in enumerate(((q_own, g_own), (q_sib, g_sib))):
        split_heads(q, qs.at[group])
        split_heads(g, gs.at[group])
    m_ref[...] = jnp.full_like(m_ref, NEG)
    l_ref[...] = jnp.zeros_like(l_ref)
    d_ref[...] = jnp.zeros_like(d_ref)

    def visit(tile, group, q, g, diagonal):
        k = keys[tile].reshape(TILE, width)
        for r in range(ROWS // CHUNK):
            rs = pl.ds(r * CHUNK, CHUNK)
            s = lax.dot_general(k, q[rs, :], NT, preferred_element_type=jnp.float32)
            dp = lax.dot_general(k[:, :lat], g[rs, :], NT, preferred_element_type=jnp.float32)
            s = jnp.concatenate(masked(info, s, group, tile, diagonal, parts), axis=0)
            s = s.reshape(TILE // 8, 8, CHUNK)
            dp = dp.reshape(TILE // 8, 8, CHUNK)
            before = m_ref[group, :, rs]
            top = jnp.maximum(before, jnp.max(s, axis=0))
            shrink = jnp.exp2((before - top) * EXP2_SCALE)
            p = jnp.exp2((s - top[None]) * EXP2_SCALE)
            m_ref[group, :, rs] = top
            l_ref[group, :, rs] = l_ref[group, :, rs] * shrink + jnp.sum(p, axis=0)
            d_ref[group, :, rs] = d_ref[group, :, rs] * shrink + jnp.sum(p * dp, axis=0)

    def step(tile, diagonal):
        wait_keys(info, kv, keys, sem, tile)
        for group in range(2):
            @pl.when(tile_used(info, group, tile))
            def _(group=group):
                visit(tile, group, qs.at[group], gs.at[group], diagonal and group == 0)

    first, last = tile_span(info)

    def body(tile, _):
        step(tile, False)
        return 0

    lax.fori_loop(first, last, body, 0)
    step(last, True)

    for group in range(2):
        m, l, d = m_ref[group], l_ref[group], d_ref[group]
        top = jnp.max(m, axis=0, keepdims=True)
        weight = jnp.exp2((m - top) * EXP2_SCALE)
        out[group, 0:1, :] = top
        out[group, 1:2, :] = jnp.sum(l * weight, axis=0, keepdims=True)
        out[group, 2:3, :] = jnp.sum(d * weight, axis=0, keepdims=True)
        out[group, 3:8, :] = jnp.zeros((5, ROWS), jnp.float32)


def grad_kernel(parts, info, q_own, q_sib, g_own, g_sib, mine, theirs, *refs):
    kv = refs[:parts]
    dq_own, dq_sib = refs[parts:parts + 2]
    far = refs[parts + 2:2 * parts + 2]
    qs, gs, keys, acc, norm, total, stage, zero, sem, z_sem, o_sem = refs[2 * parts + 2:]
    width, lat = qs.shape[2], gs.shape[2]
    tiles = keys.shape[0]
    load_keys(info, kv, keys, sem)
    first, last = tile_span(info)
    zero[...] = jnp.zeros_like(zero)

    def zero_copies(tile):
        return each_copy(info, far, zero, z_sem.at[tile], tile, True)

    def begin_zero(tile, _):
        for copy in zero_copies(tile):
            copy.start()
        return 0

    lax.fori_loop(0, first, begin_zero, 0)
    lax.fori_loop(last + 1, tiles, begin_zero, 0)
    acc[...] = jnp.zeros_like(acc)

    for group, (q, g) in enumerate(((q_own, g_own), (q_sib, g_sib))):
        split_heads(q, qs.at[group])
        split_heads(g, gs.at[group])
        a, b = mine[group], theirs[1 - group]
        top = jnp.maximum(a[0:1], b[0:1])
        wa = jnp.exp2((a[0:1] - top) * EXP2_SCALE)
        wb = jnp.exp2((b[0:1] - top) * EXP2_SCALE)
        whole = a[1:2] * wa + b[1:2] * wb
        norm[group, 0:1, :] = top * EXP2_SCALE + jnp.log2(whole)
        norm[group, 1:2, :] = (a[2:3] * wa + b[2:3] * wb) / whole

    def visit(tile, group, q, g, diagonal):
        k = keys[tile].reshape(TILE, width)
        p_all, ds_all = [], []
        for r in range(ROWS // CHUNK):
            rs = pl.ds(r * CHUNK, CHUNK)
            s = lax.dot_general(k, q[rs, :], NT, preferred_element_type=jnp.float32)
            dp = lax.dot_general(k[:, :lat], g[rs, :], NT, preferred_element_type=jnp.float32)
            s = jnp.concatenate(masked(info, s, group, tile, diagonal, parts), axis=0)
            p = jnp.exp2(s * EXP2_SCALE - norm[group, 0:1, rs])
            ds = (p * (dp - norm[group, 1:2, rs])).astype(jnp.bfloat16)
            p_all.append(p.astype(jnp.bfloat16))
            ds_all.append(ds)
            acc[group, rs, :] += lax.dot_general(ds, k, TN, preferred_element_type=jnp.float32)
        ds = jnp.concatenate(ds_all, axis=1)
        p = jnp.concatenate(p_all, axis=1)
        dk = jnp.dot(ds, q[...], preferred_element_type=jnp.float32) * SCALE
        dv = jnp.dot(p, g[...], preferred_element_type=jnp.float32)
        return dk, dv

    def step(tile, diagonal):
        slot = lax.rem(tile - first, 2)
        wait_keys(info, kv, keys, sem, tile)

        @pl.when(tile - first >= 2)
        def _():
            for copy in out_copies(tile - 2, slot):
                copy.wait()

        total[...] = jnp.zeros_like(total)
        for group in range(2):
            @pl.when(tile_used(info, group, tile))
            def _(group=group):
                dk, dv = visit(tile, group, qs.at[group], gs.at[group], diagonal and group == 0)
                total[:, :lat] += dk[:, :lat] + dv
                total[:, lat:] += dk[:, lat:]
        stage[slot] = total[...].astype(jnp.bfloat16).reshape(stage.shape[1:])
        for copy in out_copies(tile, slot):
            copy.start()

    def out_copies(tile, slot):
        return each_copy(info, far, stage.at[slot], o_sem.at[slot], tile, True)

    def body(tile, _):
        step(tile, False)
        return 0

    lax.fori_loop(first, last, body, 0)
    step(last, True)
    join_heads(acc.at[0], dq_own)
    join_heads(acc.at[1], dq_sib)

    @pl.when(last - first >= 1)
    def _():
        for copy in out_copies(last - 1, lax.rem(last - 1 - first, 2)):
            copy.wait()

    for copy in out_copies(last, lax.rem(last - first, 2)):
        copy.wait()

    def end_zero(tile, _):
        for copy in zero_copies(tile):
            copy.wait()
        return 0

    lax.fori_loop(0, first, end_zero, 0)
    lax.fori_loop(last + 1, tiles, end_zero, 0)


def call_params():
    return pltpu.CompilerParams(vmem_limit_bytes=48 * 2**20)


def vmem():
    return pl.BlockSpec(memory_space=pltpu.VMEM)


def stats(info, rows, kv):
    parts = len(kv)
    piece, width = kv[0].shape[3:]
    lat = rows[2].shape[1] * BLK // ROWS
    tiles = 2 * kv[0].shape[2]
    return pl.pallas_call(
        lambda *refs: stats_kernel(parts, *refs),
        out_shape=jax.ShapeDtypeStruct((2, 8, ROWS), jnp.float32),
        in_specs=[pl.BlockSpec(memory_space=pltpu.SMEM)] + [vmem()] * 4
        + [pl.BlockSpec(memory_space=pl.ANY)] * parts,
        out_specs=vmem(),
        scratch_shapes=[
            pltpu.VMEM((2, ROWS, width), jnp.bfloat16),
            pltpu.VMEM((2, ROWS, lat), jnp.bfloat16),
            pltpu.VMEM((tiles, 2, parts, 4, piece, width), jnp.bfloat16),
            pltpu.VMEM((2, 8, ROWS), jnp.float32),
            pltpu.VMEM((2, 8, ROWS), jnp.float32),
            pltpu.VMEM((2, 8, ROWS), jnp.float32),
            pltpu.SemaphoreType.DMA((tiles, 2, parts)),
        ],
        compiler_params=call_params(),
        name="stats",
    )(info, *rows, *kv)


def gradients(info, rows, mine, theirs, kv):
    parts = len(kv)
    piece, width = kv[0].shape[3:]
    lat = rows[2].shape[1] * BLK // ROWS
    tiles = 2 * kv[0].shape[2]
    some = pl.BlockSpec(memory_space=pl.ANY)
    return pl.pallas_call(
        lambda *refs: grad_kernel(parts, *refs),
        out_shape=[jax.ShapeDtypeStruct(rows[0].shape, jnp.bfloat16)] * 2
        + [jax.ShapeDtypeStruct(k.shape, jnp.bfloat16) for k in kv],
        in_specs=[pl.BlockSpec(memory_space=pltpu.SMEM)] + [vmem()] * 6 + [some] * parts,
        out_specs=[vmem()] * 2 + [some] * parts,
        scratch_shapes=[
            pltpu.VMEM((2, ROWS, width), jnp.bfloat16),
            pltpu.VMEM((2, ROWS, lat), jnp.bfloat16),
            pltpu.VMEM((tiles, 2, parts, 4, piece, width), jnp.bfloat16),
            pltpu.VMEM((2, ROWS, width), jnp.float32),
            pltpu.VMEM((2, 8, ROWS), jnp.float32),
            pltpu.VMEM((TILE, width), jnp.float32),
            pltpu.VMEM((2, 2, parts, 4, piece, width), jnp.bfloat16),
            pltpu.VMEM((2, parts, 4, piece, width), jnp.bfloat16),
            pltpu.SemaphoreType.DMA((tiles, 2, parts)),
            pltpu.SemaphoreType.DMA((tiles, 2, parts)),
            pltpu.SemaphoreType.DMA((2, 2, parts)),
        ],
        compiler_params=call_params(),
        name="gradients",
    )(info, *rows, mine, theirs, *kv)

EXPERTS = 256
ROUTE_SCALE = 2.5
Z_NEAR, Y_RING, CORES, X_RING, Z_FAR = 8, 4, 2, 4, 2
REACH = 4


def around(value, axis, steps, count=4):
    return lax.ppermute(value, axis, [(i, (i + steps) % count) for i in range(count)])


def along_z(value, steps):
    pairs = [(i, i + steps) for i in range(Z_NEAR) if 0 <= i + steps < Z_NEAR]
    return lax.ppermute(value, "z", pairs)


def other_core(value):
    return around(value, "core", 1, CORES)


def plus(*terms):
    return sum(t.astype(jnp.float32) for t in terms).astype(jnp.bfloat16)


def ring_gather(mine, axis):
    half = mine.shape[0] // 2
    up, down = around(mine, axis, 1), around(mine, axis, -1)
    first, second = around(up[:half], axis, 1), around(down[half:], axis, -1)
    return jnp.stack([mine, down, jnp.concatenate([first, second]), up])


def short_gather(mine, axis):
    return jnp.stack([mine, around(mine, axis, -1), around(mine, axis, 2), around(mine, axis, 1)])


def ring_reduce(terms, axis):
    half = terms.shape[1] // 2
    first, second = around(terms[2, :half], axis, 1), around(terms[2, half:], axis, -1)
    up = jnp.concatenate([plus(terms[1, :half], first), terms[1, half:]])
    down = jnp.concatenate([terms[3, :half], plus(terms[3, half:], second)])
    return plus(terms[0], around(up, axis, 1), around(down, axis, -1))


def short_reduce(terms, axis):
    return plus(terms[0], around(terms[1], axis, 1), around(terms[2], axis, 2), around(terms[3], axis, -1))


def gather_keys(latents):
    quarter = latents.shape[0] // X_RING
    piece = lax.dynamic_slice_in_dim(latents, lax.axis_index("x") * quarter, quarter, 0)
    planes = jnp.stack([along_z(piece, REACH - p) for p in range(REACH)] + [piece])
    half = quarter // 2
    return [
        ring_gather(short_gather(planes[:, :half], "x"), "y"),
        ring_gather(short_gather(planes[:, half:], "y"), "x"),
    ]


def return_grads(terms):
    first = short_reduce(ring_reduce(terms[0], "y"), "x")
    second = short_reduce(ring_reduce(terms[1], "x"), "y")
    planes = jnp.concatenate([first, second], axis=1)
    total = planes[REACH].astype(jnp.float32)
    for p in range(REACH):
        total = total + along_z(planes[p], p - REACH).astype(jnp.float32)
    total = total + around(total.astype(jnp.bfloat16), "far", 1, Z_FAR).astype(jnp.float32)
    return lax.all_gather(total.astype(jnp.bfloat16), "x", tiled=True)


def attention_part(queries, latents, out_grad, block_start):
    z, y, core, x = (lax.axis_index(a) for a in ("z", "y", "core", "x"))
    kv = gather_keys(latents)
    rows = [queries, other_core(queries), out_grad, other_core(out_grad)]
    starts = jnp.stack([block_start[0], other_core(block_start)[0]]) - 2 * Y_RING * (z - REACH)
    lows = (starts - core + 1) // 2
    own = REACH * Y_RING + y
    info = jnp.stack([lows[0], lows[1], own - core, own, y, x]).astype(jnp.int32)
    mine = stats(info, rows, kv)
    grads = gradients(info, rows, mine, other_core(mine), kv)
    return plus(grads[0], other_core(grads[1])), return_grads(grads[2:])


def routing_part(moe_grad, affinity, expert_ids, expert_out):
    tokens, top = expert_ids.shape
    groups = X_RING * Z_FAR
    saved = expert_out[0, 0]
    capacity = saved.shape[1]
    every = lax.all_gather(moe_grad, ("x", "far"))
    terms = jnp.einsum("scd,std->sct", saved, every, preferred_element_type=jnp.float32)
    gathered = lax.all_gather(terms.reshape(groups, -1), ("x", "far"))
    me = lax.axis_index("x") * Z_FAR + lax.axis_index("far")
    back = lax.dynamic_index_in_dim(gathered, me, 1, keepdims=False)
    owner = (expert_ids // (EXPERTS // groups)).reshape(-1)
    order = jnp.arange(tokens * top, dtype=jnp.int32)
    before = jnp.logical_and(owner[:, None] == owner[None, :], order[:, None] > order[None, :])
    slot = jnp.sum(before.astype(jnp.int32), axis=1)
    place = (owner * capacity + slot).reshape(tokens, top)
    table = back.reshape(groups * capacity, tokens).T
    chosen = place[:, :, None] == jnp.arange(groups * capacity, dtype=jnp.int32)
    gate_grad = jnp.sum(jnp.where(chosen, table[:, None, :], 0.0), axis=2)
    total = jnp.sum(affinity, axis=1, keepdims=True)
    weighted = jnp.sum(gate_grad * affinity, axis=1, keepdims=True) / total
    return ROUTE_SCALE / total * (gate_grad - weighted) * affinity * (1.0 - affinity)


def local(queries, latents, out_grad, block_start, moe_grad, affinity, expert_ids, expert_out):
    query_grad, latent_grad = attention_part(queries, latents, out_grad, block_start)
    logit_grad = routing_part(moe_grad, affinity, expert_ids, expert_out)
    return (query_grad, latent_grad, logit_grad)


def solution(mesh):
    parts = mesh.devices.reshape(Z_NEAR, Y_RING, CORES, X_RING, Z_FAR)
    grid = Mesh(parts, ("z", "y", "core", "x", "far"))
    ctx, exp = ("z", "y", "core"), ("x", "far")
    in_specs = (
        P(ctx, exp),
        P(ctx, None),
        P(ctx, exp),
        P(ctx),
        P(ctx + exp, None),
        P(ctx + exp, None),
        P(ctx + exp, None),
        P(ctx, exp, None, None, None),
    )
    out_specs = (P(ctx, exp), P(ctx, None), P(ctx + exp, None))
    return jax.shard_map(local, mesh=grid, in_specs=in_specs, out_specs=out_specs, check_vma=False)
```

```python
import jax
import jax.numpy as jnp
import numpy as np
from jax import lax
from jax.experimental import pallas as pl
from jax.experimental.pallas import tpu as pltpu
from jax.sharding import Mesh, PartitionSpec as P

SCALE = 192.0 ** (-0.5)
EXP2_SCALE = SCALE * 1.4426950408889634
NEG = -1e30
BLK = 128
TILE = 2 * BLK
CHUNK = 512
ROWS = 8 * BLK
NT = (((1,), (1,)), ((), ()))
TN = (((0,), (0,)), ((), ()))


def piece_places(info, tile):
    places = []
    for half in range(2):
        block = 2 * tile + half
        plane, turn = block >> 2, (block + 4 - info[4]) & 3
        first = jnp.where(info[6] == 0, turn * 20, turn * 5) + plane
        step = jnp.where(info[6] == 0, 5, 20)
        places += [first + i * step for i in range(4)]
    return places


def tile_keys(info, keys, tile):
    return jnp.concatenate([keys[place] for place in piece_places(info, tile)], axis=0)


def tile_span(info):
    own = info[3]
    last = own // 2
    first = jnp.minimum(jnp.minimum(info[0], info[1]) // 2, last)
    return first, last


def row_limits(info, group):
    return (info[0], info[3]) if group == 0 else (info[1], info[2])


def block_bias(info, group, tile):
    low, high = row_limits(info, group)
    return [jnp.where(jnp.logical_and(2 * tile + half >= low, 2 * tile + half <= high), 0.0, NEG)
            for half in range(2)]


def tile_used(info, group, tile):
    low, high = row_limits(info, group)
    return jnp.logical_and(2 * tile + 1 >= low, jnp.logical_and(2 * tile <= high, low <= high))


def column_bias(info, group, tile):
    first, second = block_bias(info, group, tile)
    place = lax.broadcasted_iota(jnp.int32, (1, TILE), 1)
    return jnp.where(place < BLK, first, second)


def later_keys(info, tile, s, row_start):
    place = lax.broadcasted_iota(jnp.int32, s.shape, 1)
    row = (lax.broadcasted_iota(jnp.int32, s.shape, 0) + row_start) % BLK
    size = BLK // 4
    within = place % BLK
    key = (within // size + info[5]) % 4 * size + within % size
    own = 2 * tile + place // BLK == info[3]
    return jnp.where(jnp.logical_and(own, key > row), NEG, s)


def masked_columns(info, s, group, tile, diagonal):
    bias = block_bias(info, group, tile)
    halves = []
    for half in range(2):
        part = s[half * BLK:(half + 1) * BLK] + bias[half]
        if diagonal:
            place = lax.broadcasted_iota(jnp.int32, part.shape, 0)
            row = lax.broadcasted_iota(jnp.int32, part.shape, 1) % BLK
            size = BLK // 4
            key = (place // size + info[5]) % 4 * size + place % size
            later = jnp.logical_and(key > row, info[3] == 2 * tile + half)
            part = jnp.where(later, NEG, part)
        halves.append(part)
    return halves[0], halves[1]


def split_heads(rows, heads):
    width = heads.shape[1]
    for pair in range(ROWS // BLK // 2):
        both = rows[:BLK, 2 * width * pair:2 * width * (pair + 1)]
        heads[pl.ds(2 * pair * BLK, BLK), :] = both[:, :width]
        heads[pl.ds((2 * pair + 1) * BLK, BLK), :] = both[:, width:]


def join_heads(heads, rows):
    width = heads.shape[1]
    for pair in range(ROWS // BLK // 2):
        both = [heads[pl.ds((2 * pair + i) * BLK, BLK), :] * SCALE for i in range(2)]
        rows[:, 2 * width * pair:2 * width * (pair + 1)] = jnp.concatenate(both, axis=1).astype(rows.dtype)


def stats_kernel(info, q_own, q_sib, g_own, g_sib, *refs):
    out, keys, qs, gs, m_ref, l_ref, d_ref = refs[4:]
    width, lat = qs.shape[2], gs.shape[2]
    for i, pieces in enumerate(refs[:4]):
        keys[pl.ds(i * 20, 20)] = pieces[...].reshape((20,) + pieces.shape[2:])
    for group, (q, g) in enumerate(((q_own, g_own), (q_sib, g_sib))):
        split_heads(q, qs.at[group])
        split_heads(g, gs.at[group])
    m_ref[...] = jnp.full_like(m_ref, NEG)
    l_ref[...] = jnp.zeros_like(l_ref)
    d_ref[...] = jnp.zeros_like(d_ref)

    def visit(tile, group, q, g, diagonal):
        k = tile_keys(info, keys, tile)
        for r in range(ROWS // CHUNK):
            rs = pl.ds(r * CHUNK, CHUNK)
            s = lax.dot_general(k, q[rs, :], NT, preferred_element_type=jnp.float32)
            dp = lax.dot_general(k[:, :lat], g[rs, :], NT, preferred_element_type=jnp.float32)
            s = jnp.concatenate(masked_columns(info, s, group, tile, diagonal), axis=0)
            s = s.reshape(TILE // 8, 8, CHUNK)
            dp = dp.reshape(TILE // 8, 8, CHUNK)
            before = m_ref[group, :, rs]
            top = jnp.maximum(before, jnp.max(s, axis=0))
            shrink = jnp.exp2((before - top) * EXP2_SCALE)
            p = jnp.exp2((s - top[None]) * EXP2_SCALE)
            m_ref[group, :, rs] = top
            l_ref[group, :, rs] = l_ref[group, :, rs] * shrink + jnp.sum(p, axis=0)
            d_ref[group, :, rs] = d_ref[group, :, rs] * shrink + jnp.sum(p * dp, axis=0)

    def step(tile, diagonal):
        for group in range(2):
            @pl.when(tile_used(info, group, tile))
            def _(group=group):
                visit(tile, group, qs.at[group], gs.at[group], diagonal and group == 0)

    first, last = tile_span(info)

    def body(tile, _):
        step(tile, False)
        return 0

    lax.fori_loop(first, last, body, 0)
    step(last, True)

    for group in range(2):
        m, l, d = m_ref[group], l_ref[group], d_ref[group]
        top = jnp.max(m, axis=0, keepdims=True)
        weight = jnp.exp2((m - top) * EXP2_SCALE)
        out[group, 0:1, :] = top
        out[group, 1:2, :] = jnp.sum(l * weight, axis=0, keepdims=True)
        out[group, 2:3, :] = jnp.sum(d * weight, axis=0, keepdims=True)
        out[group, 3:8, :] = jnp.zeros((5, ROWS), jnp.float32)


def grad_kernel(info, keys, qs, gs, mine, theirs, dq_own, dq_sib, *refs):
    qt, gt, acc, norm, total, sums = refs[4:]
    width, lat = qs.shape[2], gs.shape[2]
    first, last = tile_span(info)
    sums[...] = jnp.zeros_like(sums)
    acc[...] = jnp.zeros_like(acc)

    for group in range(2):
        a, b = mine[group], theirs[1 - group]
        top = jnp.maximum(a[0:1], b[0:1])
        wa = jnp.exp2((a[0:1] - top) * EXP2_SCALE)
        wb = jnp.exp2((b[0:1] - top) * EXP2_SCALE)
        whole = a[1:2] * wa + b[1:2] * wb
        level = top * EXP2_SCALE + jnp.log2(whole)
        delta = (a[2:3] * wa + b[2:3] * wb) / whole
        for h in range(ROWS // BLK):
            cs = slice(h * BLK, (h + 1) * BLK)
            rs = pl.ds(h * BLK, BLK)
            norm[0, group, rs, :] = jnp.broadcast_to(level[:, cs], (BLK, BLK)).T
            norm[1, group, rs, :] = jnp.broadcast_to(delta[:, cs], (BLK, BLK)).T
            qt[group, :, cs] = qs[group, rs, :].T
            gt[group, :, cs] = gs[group, rs, :].T

    def visit(tile, group, diagonal):
        k = tile_keys(info, keys, tile)
        bias = column_bias(info, group, tile)
        p_all, ds_all = [], []
        for r in range(ROWS // CHUNK):
            rs = pl.ds(r * CHUNK, CHUNK)
            s = lax.dot_general(qs[group, rs, :], k, NT, preferred_element_type=jnp.float32) + bias
            dp = lax.dot_general(gs[group, rs, :], k[:, :lat], NT, preferred_element_type=jnp.float32)
            if diagonal:
                s = later_keys(info, tile, s, r * CHUNK)
            level, delta = norm[0, group, rs, :], norm[1, group, rs, :]
            p, ds = [], []
            for h in range(2):
                cs = slice(h * BLK, (h + 1) * BLK)
                prob = jnp.exp2(s[:, cs] * EXP2_SCALE - level)
                ds.append((prob * (dp[:, cs] - delta)).astype(jnp.bfloat16))
                p.append(prob.astype(jnp.bfloat16))
            ds = jnp.concatenate(ds, axis=1)
            acc[group, rs, :] += jnp.dot(ds, k, preferred_element_type=jnp.float32)
            p_all.append(jnp.concatenate(p, axis=1))
            ds_all.append(ds)
        ds, p = jnp.concatenate(ds_all, axis=0), jnp.concatenate(p_all, axis=0)
        dk = jnp.dot(qt[group], ds, preferred_element_type=jnp.float32) * SCALE
        dv = jnp.dot(gt[group], p, preferred_element_type=jnp.float32)
        total[:lat, :] += dk[:lat] + dv
        total[lat:, :] += dk[lat:]

    def step(tile, diagonal):
        total[...] = jnp.zeros_like(total)
        for group in range(2):
            @pl.when(tile_used(info, group, tile))
            def _(group=group):
                visit(tile, group, diagonal and group == 0)
        rows = total[...].T.astype(jnp.bfloat16).reshape((8, -1, width))
        for i, place in enumerate(piece_places(info, tile)):
            sums[place] = rows[i]

    def body(tile, _):
        step(tile, False)
        return 0

    lax.fori_loop(first, last, body, 0)
    step(last, True)
    join_heads(acc.at[0], dq_own)
    join_heads(acc.at[1], dq_sib)

    for i, pieces in enumerate(refs[:4]):
        pieces[...] = sums[pl.ds(i * 20, 20)].reshape(pieces.shape)


def call_params():
    return pltpu.CompilerParams(vmem_limit_bytes=40 * 2**20)


def vmem(count):
    return [pl.BlockSpec(memory_space=pltpu.VMEM)] * count


def stats(info, rows, kv):
    planes, piece, width = kv[0].shape[1:]
    lat = rows[2].shape[1] * BLK // ROWS
    low = jnp.bfloat16
    return pl.pallas_call(
        stats_kernel,
        out_shape=[
            jax.ShapeDtypeStruct((2, 8, ROWS), jnp.float32),
            jax.ShapeDtypeStruct((16 * planes, piece, width), low),
            jax.ShapeDtypeStruct((2, ROWS, width), low),
            jax.ShapeDtypeStruct((2, ROWS, lat), low),
        ],
        in_specs=[pl.BlockSpec(memory_space=pltpu.SMEM)] + vmem(8),
        out_specs=vmem(4),
        scratch_shapes=[pltpu.VMEM((2, 8, ROWS), jnp.float32)] * 3,
        compiler_params=call_params(),
        cost_estimate=pl.CostEstimate(flops=10 * 10**9, bytes_accessed=10**7, transcendentals=10**7),
        name="stats",
    )(info, *rows, *kv)


def gradients(info, keys, qs, gs, mine, theirs):
    width, lat = qs.shape[2], gs.shape[2]
    planes, piece = keys.shape[0] // 16, keys.shape[1]
    low = jnp.bfloat16
    return pl.pallas_call(
        grad_kernel,
        out_shape=[jax.ShapeDtypeStruct((BLK, ROWS // BLK * width), low)] * 2
        + [jax.ShapeDtypeStruct((4, planes, piece, width), low)] * 4,
        in_specs=[pl.BlockSpec(memory_space=pltpu.SMEM)] + vmem(5),
        out_specs=vmem(6),
        scratch_shapes=[
            pltpu.VMEM((2, width, ROWS), low),
            pltpu.VMEM((2, lat, ROWS), low),
            pltpu.VMEM((2, ROWS, width), jnp.float32),
            pltpu.VMEM((2, 2, ROWS, BLK), jnp.float32),
            pltpu.VMEM((width, TILE), jnp.float32),
            pltpu.VMEM(keys.shape, low),
        ],
        compiler_params=call_params(),
        cost_estimate=pl.CostEstimate(flops=25 * 10**9, bytes_accessed=10**7, transcendentals=10**7),
        name="gradients",
    )(info, keys, qs, gs, mine, theirs)

EXPERTS = 256
ROUTE_SCALE = 2.5
Z_NEAR, Y_RING, CORES, X_RING, Z_FAR = 8, 4, 2, 4, 2
REACH = 4
GRID = ("z", "y", "core", "x", "far")


def around(value, axis, steps, count=4):
    return lax.ppermute(value, axis, [(i, (i + steps) % count) for i in range(count)])


def along_z(value, steps):
    pairs = [(i, i + steps) for i in range(Z_NEAR) if 0 <= i + steps < Z_NEAR]
    return lax.ppermute(value, "z", pairs)


def other_core(value):
    return around(value, "core", 1, CORES)


def plus(*terms):
    return sum(t.astype(jnp.float32) for t in terms).astype(jnp.bfloat16)


def in_plane(value, stage, steps):
    pairs = []
    for place in np.ndindex(Z_NEAR, Y_RING, CORES, X_RING, Z_FAR):
        there = list(place)
        axis = 3 if place[2] == stage else 1
        there[axis] = (there[axis] + steps) % 4
        pairs.append(tuple(int(np.ravel_multi_index(p, (Z_NEAR, Y_RING, CORES, X_RING, Z_FAR))) for p in (place, there)))
    return lax.ppermute(value, GRID, pairs)


def gather_keys(latents):
    quarter = latents.shape[0] // X_RING
    piece = lax.dynamic_slice_in_dim(latents, lax.axis_index("x") * quarter, quarter, 0)
    planes = jnp.stack([along_z(piece, REACH - p) for p in range(REACH)] + [piece])
    line = jnp.stack([planes, in_plane(planes, 0, -1), in_plane(planes, 0, 2), in_plane(planes, 0, 1)])
    up, down = in_plane(line, 1, 1), in_plane(line, 1, -1)
    return [line, down, in_plane(up, 1, 1), up]


def reduce_in_plane(terms):
    far = plus(terms[1], in_plane(terms[2], 1, 1))
    line = plus(terms[0], in_plane(far, 1, 1), in_plane(terms[3], 1, -1))
    return plus(line[0], in_plane(line[1], 0, 1), in_plane(line[2], 0, 2), in_plane(line[3], 0, -1)), far


def reduce_along_z(planes):
    total = planes[REACH].astype(jnp.float32)
    for p in range(REACH):
        total = total + along_z(planes[p], p - REACH).astype(jnp.float32)
    return total


def after(value, event):
    return lax.optimization_barrier((value, event))[0]


def with_start(rows, block_start):
    start = jnp.full((16, rows.shape[1]), block_start[0].astype(rows.dtype))
    return jnp.concatenate([rows, start])


def attention_info(block_start, sibling_start):
    z, y, core, x = (lax.axis_index(a) for a in ("z", "y", "core", "x"))
    starts = jnp.stack([block_start[0], sibling_start.astype(jnp.int32)]) - 2 * Y_RING * (z - REACH)
    lows = (starts - core + 1) // 2
    own = REACH * Y_RING + y
    return jnp.stack([lows[0], lows[1], own - core, own, y, x, core]).astype(jnp.int32)


def partner(value, bit):
    if bit == 0:
        return around(value, "far", 1, Z_FAR)
    return lax.ppermute(value, "x", [(i, (i ^ 1) if bit == 1 else 3 - i) for i in range(X_RING)])


def position(x, far):
    return (x ^ (x // 2)) * 2 + far


def gate_products(every, expert_out, me):
    saved = expert_out[0, 0]
    products = [jnp.einsum("scd,rtd->srct", saved, rows, preferred_element_type=jnp.float32) for rows in every]
    products = jnp.concatenate(products, axis=1)
    group = jnp.arange(X_RING * Z_FAR, dtype=jnp.int32)
    apart = position(group // Z_FAR, group % Z_FAR) ^ me
    same = apart[:, None] == group[None, :]
    terms = jnp.sum(jnp.where(same[:, :, None, None], products, 0.0), axis=0)
    return terms.reshape(X_RING, Z_FAR, -1)


def letter(rows, gates):
    high = gates.astype(jnp.bfloat16)
    rest = (gates - high.astype(jnp.float32)).astype(jnp.bfloat16)
    both = jnp.concatenate([high, rest])
    room = ((0, 16 - both.shape[0]), (0, rows.shape[1] - both.shape[1]))
    return jnp.concatenate([rows, jnp.pad(both, room)])


def opened(mail, count, size):
    both = mail[-16:, :size].astype(jnp.float32)
    return mail[:-16], both[:count] + both[count:2 * count]


def settle(part, gates):
    size = gates.shape[2]
    x = lax.axis_index("x")
    mail = around(letter(part.astype(jnp.bfloat16), gates[:, 1]), "far", 1, Z_FAR)
    rows, theirs = opened(mail, X_RING, size)
    whole = plus(part, rows)
    gates = jnp.stack([gates[:, 0], theirs], axis=1)
    even = x % 2 == 0
    ahead, behind = jnp.where(even, gates[1], gates[2]), jnp.where(even, gates[2], gates[1])
    mails = [
        around(letter(whole, behind), "x", -1),
        around(letter(whole, gates[3]), "x", 2),
        around(letter(whole, ahead), "x", 1),
    ]
    (r1, g1), (r2, g2), (r3, g3) = [opened(mail, Z_FAR, size) for mail in mails]
    twice = jnp.stack([whole, r1, r2, r3, whole, r1, r2, r3])
    block = lax.dynamic_slice_in_dim(twice, (X_RING - x) % X_RING, X_RING, 0)
    gates = jnp.stack([gates[0], jnp.where(even, g1, g3), jnp.where(even, g3, g1), g2])
    return block.reshape(-1, block.shape[2]), gates.reshape(X_RING * Z_FAR, size)


def logit_part(gates, affinity, expert_ids, me):
    tokens, top = expert_ids.shape
    groups, size = gates.shape
    owner = (expert_ids // (EXPERTS // groups)).reshape(-1)
    order = jnp.arange(tokens * top, dtype=jnp.int32)
    before = jnp.logical_and(owner[:, None] == owner[None, :], order[:, None] > order[None, :])
    slot = jnp.sum(before.astype(jnp.int32), axis=1)
    there = position(owner // Z_FAR, owner % Z_FAR) ^ me
    place = (there * size + slot * tokens + order // top).reshape(tokens, top)
    index = jnp.arange(groups * size, dtype=jnp.int32).reshape(groups, size)
    chosen = place[:, :, None, None] == index
    gate_grad = jnp.sum(jnp.where(chosen, gates, 0.0), axis=(2, 3))
    total = jnp.sum(affinity, axis=1, keepdims=True)
    weighted = jnp.sum(gate_grad * affinity, axis=1, keepdims=True) / total
    return ROUTE_SCALE / total * (gate_grad - weighted) * affinity * (1.0 - affinity)


def local(queries, latents, out_grad, block_start, moe_grad, affinity, expert_ids, expert_out):
    kv = gather_keys(latents)
    sibling_grad = other_core(with_start(out_grad, block_start))
    rows = [queries, other_core(queries), out_grad, sibling_grad]
    me = position(lax.axis_index("x"), lax.axis_index("far"))
    two = jnp.stack([moe_grad, partner(moe_grad, 0)])
    info = attention_info(block_start, sibling_grad[out_grad.shape[0], 0])
    four = jnp.concatenate([two, partner(after(two, kv[2]), 1)])
    mine, *prepared = stats(info, rows, kv)
    every = [four, partner(after(four, mine), 2)]
    own, sibling, *terms = gradients(info, *prepared, mine, other_core(mine))
    planes, middle = reduce_in_plane(terms)
    query_grad = plus(own, other_core(after(sibling, middle)))
    gates = gate_products(every, after(expert_out, middle), me)
    latent_grad, gates = settle(reduce_along_z(planes), gates)
    return (query_grad, latent_grad, logit_part(gates, affinity, expert_ids, me))


def solution(mesh):
    parts = mesh.devices.reshape(Z_NEAR, Y_RING, CORES, X_RING, Z_FAR)
    grid = Mesh(parts, GRID)
    ctx, exp = GRID[:3], GRID[3:]
    in_specs = (
        P(ctx, exp),
        P(ctx, None),
        P(ctx, exp),
        P(ctx),
        P(ctx + exp, None),
        P(ctx + exp, None),
        P(ctx + exp, None),
        P(ctx, exp, None, None, None),
    )
    out_specs = (P(ctx, exp), P(ctx, None), P(ctx + exp, None))
    return jax.shard_map(local, mesh=grid, in_specs=in_specs, out_specs=out_specs, check_vma=False)
```

```python
import jax
import jax.numpy as jnp
import numpy as np
from jax import lax
from jax.experimental import pallas as pl
from jax.experimental.pallas import tpu as pltpu
from jax.sharding import Mesh, PartitionSpec as P

SCALE = 192.0 ** (-0.5)
EXP2_SCALE = SCALE * 1.4426950408889634
NEG = -1e30
BLK = 128
TILE = 2 * BLK
CHUNK = 512
ROWS = 8 * BLK
NT = (((1,), (1,)), ((), ()))
TN = (((0,), (0,)), ((), ()))


def piece_places(info, tile):
    places = []
    for half in range(2):
        block = 2 * tile + half
        plane, turn = block >> 2, (block + 4 - info[4]) & 3
        first = jnp.where(info[6] == 0, turn * 20, turn * 5) + plane
        step = jnp.where(info[6] == 0, 5, 20)
        places += [first + i * step for i in range(4)]
    return places


def tile_keys(info, keys, tile):
    return jnp.concatenate([keys[place] for place in piece_places(info, tile)], axis=0)


def tile_span(info):
    own = info[3]
    last = own // 2
    first = jnp.minimum(jnp.minimum(info[0], info[1]) // 2, last)
    return first, last


def row_limits(info, group):
    return (info[0], info[3]) if group == 0 else (info[1], info[2])


def block_bias(info, group, tile):
    low, high = row_limits(info, group)
    return [jnp.where(jnp.logical_and(2 * tile + half >= low, 2 * tile + half <= high), 0.0, NEG)
            for half in range(2)]


def tile_used(info, group, tile):
    low, high = row_limits(info, group)
    return jnp.logical_and(2 * tile + 1 >= low, jnp.logical_and(2 * tile <= high, low <= high))


def column_bias(info, group, tile):
    first, second = block_bias(info, group, tile)
    place = lax.broadcasted_iota(jnp.int32, (1, TILE), 1)
    return jnp.where(place < BLK, first, second)


def later_keys(info, tile, s, row_start):
    place = lax.broadcasted_iota(jnp.int32, s.shape, 1)
    row = (lax.broadcasted_iota(jnp.int32, s.shape, 0) + row_start) % BLK
    size = BLK // 4
    within = place % BLK
    key = (within // size + info[5]) % 4 * size + within % size
    own = 2 * tile + place // BLK == info[3]
    return jnp.where(jnp.logical_and(own, key > row), NEG, s)


def masked_columns(info, s, group, tile, diagonal):
    bias = block_bias(info, group, tile)
    halves = []
    for half in range(2):
        part = s[half * BLK:(half + 1) * BLK] + bias[half]
        if diagonal:
            place = lax.broadcasted_iota(jnp.int32, part.shape, 0)
            row = lax.broadcasted_iota(jnp.int32, part.shape, 1) % BLK
            size = BLK // 4
            key = (place // size + info[5]) % 4 * size + place % size
            later = jnp.logical_and(key > row, info[3] == 2 * tile + half)
            part = jnp.where(later, NEG, part)
        halves.append(part)
    return halves[0], halves[1]


def split_heads(rows, heads):
    width = heads.shape[1]
    for pair in range(ROWS // BLK // 2):
        both = rows[:BLK, 2 * width * pair:2 * width * (pair + 1)]
        heads[pl.ds(2 * pair * BLK, BLK), :] = both[:, :width]
        heads[pl.ds((2 * pair + 1) * BLK, BLK), :] = both[:, width:]


def join_heads(heads, rows):
    width = heads.shape[1]
    for pair in range(ROWS // BLK // 2):
        both = [heads[pl.ds((2 * pair + i) * BLK, BLK), :] * SCALE for i in range(2)]
        rows[:, 2 * width * pair:2 * width * (pair + 1)] = jnp.concatenate(both, axis=1).astype(rows.dtype)


def prepare_kernel(q, g, qs, gs, qt, gt):
    split_heads(q, qs)
    split_heads(g, gs)
    for h in range(ROWS // BLK):
        rs = pl.ds(h * BLK, BLK)
        qt[:, h * BLK:(h + 1) * BLK] = qs[rs, :].T
        gt[:, h * BLK:(h + 1) * BLK] = gs[rs, :].T


def stats_kernel(info, q_own, g_own, q_sib, g_sib, *refs):
    *kv, out, keys, m_ref, l_ref, d_ref = refs
    width, lat = q_own.shape[1], g_own.shape[1]
    begin = 0
    for pieces in kv:
        count = pieces.shape[0] * pieces.shape[1]
        keys[pl.ds(begin, count)] = pieces[...].reshape((count,) + pieces.shape[2:])
        begin += count
    m_ref[...] = jnp.full_like(m_ref, NEG)
    l_ref[...] = jnp.zeros_like(l_ref)
    d_ref[...] = jnp.zeros_like(d_ref)

    def visit(tile, group, q, g, diagonal):
        k = tile_keys(info, keys, tile)
        for r in range(ROWS // CHUNK):
            rs = pl.ds(r * CHUNK, CHUNK)
            s = lax.dot_general(k, q[rs, :], NT, preferred_element_type=jnp.float32)
            dp = lax.dot_general(k[:, :lat], g[rs, :], NT, preferred_element_type=jnp.float32)
            s = jnp.concatenate(masked_columns(info, s, group, tile, diagonal), axis=0)
            s = s.reshape(TILE // 8, 8, CHUNK)
            dp = dp.reshape(TILE // 8, 8, CHUNK)
            before = m_ref[group, :, rs]
            top = jnp.maximum(before, jnp.max(s, axis=0))
            shrink = jnp.exp2((before - top) * EXP2_SCALE)
            p = jnp.exp2((s - top[None]) * EXP2_SCALE)
            m_ref[group, :, rs] = top
            l_ref[group, :, rs] = l_ref[group, :, rs] * shrink + jnp.sum(p, axis=0)
            d_ref[group, :, rs] = d_ref[group, :, rs] * shrink + jnp.sum(p * dp, axis=0)

    def step(tile, diagonal):
        for group, (q, g) in enumerate(((q_own, g_own), (q_sib, g_sib))):
            @pl.when(tile_used(info, group, tile))
            def _(group=group, q=q, g=g):
                visit(tile, group, q, g, diagonal and group == 0)

    first, last = tile_span(info)

    def body(tile, _):
        step(tile, False)
        return 0

    lax.fori_loop(first, last, body, 0)
    step(last, True)

    for group in range(2):
        m, l, d = m_ref[group], l_ref[group], d_ref[group]
        top = jnp.max(m, axis=0, keepdims=True)
        weight = jnp.exp2((m - top) * EXP2_SCALE)
        out[group, 0:1, :] = top
        out[group, 1:2, :] = jnp.sum(l * weight, axis=0, keepdims=True)
        out[group, 2:3, :] = jnp.sum(d * weight, axis=0, keepdims=True)
        out[group, 3:8, :] = jnp.zeros((5, ROWS), jnp.float32)


def grad_kernel(info, keys, *refs):
    rows, (mine, theirs, dq_own, dq_sib) = (refs[:4], refs[4:8]), refs[8:12]
    *terms, acc, norm, total, sums = refs[12:]
    width, lat = rows[0][0].shape[1], rows[0][1].shape[1]
    first, last = tile_span(info)
    sums[...] = jnp.zeros_like(sums)
    acc[...] = jnp.zeros_like(acc)

    for group in range(2):
        a, b = mine[group], theirs[1 - group]
        top = jnp.maximum(a[0:1], b[0:1])
        wa = jnp.exp2((a[0:1] - top) * EXP2_SCALE)
        wb = jnp.exp2((b[0:1] - top) * EXP2_SCALE)
        whole = a[1:2] * wa + b[1:2] * wb
        level = top * EXP2_SCALE + jnp.log2(whole)
        delta = (a[2:3] * wa + b[2:3] * wb) / whole
        for h in range(ROWS // BLK):
            cs = slice(h * BLK, (h + 1) * BLK)
            rs = pl.ds(h * BLK, BLK)
            norm[0, group, rs, :] = jnp.broadcast_to(level[:, cs], (BLK, BLK)).T
            norm[1, group, rs, :] = jnp.broadcast_to(delta[:, cs], (BLK, BLK)).T

    def visit(tile, group, diagonal):
        qs, gs, qt, gt = rows[group]
        k = tile_keys(info, keys, tile)
        bias = column_bias(info, group, tile)
        p_all, ds_all = [], []
        for r in range(ROWS // CHUNK):
            rs = pl.ds(r * CHUNK, CHUNK)
            s = lax.dot_general(qs[rs, :], k, NT, preferred_element_type=jnp.float32) + bias
            dp = lax.dot_general(gs[rs, :], k[:, :lat], NT, preferred_element_type=jnp.float32)
            if diagonal:
                s = later_keys(info, tile, s, r * CHUNK)
            level, delta = norm[0, group, rs, :], norm[1, group, rs, :]
            p, ds = [], []
            for h in range(2):
                cs = slice(h * BLK, (h + 1) * BLK)
                prob = jnp.exp2(s[:, cs] * EXP2_SCALE - level)
                ds.append((prob * (dp[:, cs] - delta)).astype(jnp.bfloat16))
                p.append(prob.astype(jnp.bfloat16))
            ds = jnp.concatenate(ds, axis=1)
            acc[group, rs, :] += jnp.dot(ds, k, preferred_element_type=jnp.float32)
            p_all.append(jnp.concatenate(p, axis=1))
            ds_all.append(ds)
        ds, p = jnp.concatenate(ds_all, axis=0), jnp.concatenate(p_all, axis=0)
        dk = jnp.dot(qt[...], ds, preferred_element_type=jnp.float32) * SCALE
        dv = jnp.dot(gt[...], p, preferred_element_type=jnp.float32)
        total[:lat, :] += dk[:lat] + dv
        total[lat:, :] += dk[lat:]

    def step(tile, diagonal):
        total[...] = jnp.zeros_like(total)
        for group in range(2):
            @pl.when(tile_used(info, group, tile))
            def _(group=group):
                visit(tile, group, diagonal and group == 0)
        pieces = total[...].T.astype(jnp.bfloat16).reshape((8, -1, width))
        for i, place in enumerate(piece_places(info, tile)):
            sums[place] = pieces[i]

    def body(tile, _):
        step(tile, False)
        return 0

    lax.fori_loop(first, last, body, 0)
    step(last, True)
    join_heads(acc.at[0], dq_own)
    join_heads(acc.at[1], dq_sib)

    begin = 0
    for pieces in terms:
        count = pieces.shape[0] * pieces.shape[1]
        pieces[...] = sums[pl.ds(begin, count)].reshape(pieces.shape)
        begin += count


def call_params():
    return pltpu.CompilerParams(vmem_limit_bytes=18 * 2**20)


def vmem(count):
    return [pl.BlockSpec(memory_space=pltpu.VMEM)] * count


def shaped(*shape, kind=jnp.bfloat16):
    return jax.ShapeDtypeStruct(shape, kind)


def prepare(q, g):
    heads = ROWS // BLK
    width, lat = q.shape[1] // heads, g.shape[1] // heads
    return pl.pallas_call(
        prepare_kernel,
        out_shape=[shaped(ROWS, width), shaped(ROWS, lat), shaped(width, ROWS), shaped(lat, ROWS)],
        in_specs=vmem(2),
        out_specs=vmem(4),
        compiler_params=call_params(),
        name="prepare",
    )(q, g)


def stats(info, own, sibling, kv):
    planes, piece, width = kv[0].shape[1:]
    return pl.pallas_call(
        stats_kernel,
        out_shape=[shaped(2, 8, ROWS, kind=jnp.float32), shaped(16 * planes, piece, width)],
        in_specs=[pl.BlockSpec(memory_space=pltpu.SMEM)] + vmem(4 + len(kv)),
        out_specs=vmem(2),
        scratch_shapes=[pltpu.VMEM((2, 8, ROWS), jnp.float32)] * 3,
        compiler_params=call_params(),
        cost_estimate=pl.CostEstimate(flops=10 * 10**9, bytes_accessed=10**7, transcendentals=10**7),
        name="stats",
    )(info, *own[:2], *sibling[:2], *kv)


def gradients(info, keys, own, sibling, mine, theirs, counts):
    width = own[0].shape[1]
    planes, piece = keys.shape[0] // 16, keys.shape[1]
    return pl.pallas_call(
        grad_kernel,
        out_shape=[shaped(BLK, ROWS // BLK * width)] * 2 + [shaped(n, planes, piece, width) for n in counts],
        in_specs=[pl.BlockSpec(memory_space=pltpu.SMEM)] + vmem(11),
        out_specs=vmem(2 + len(counts)),
        scratch_shapes=[
            pltpu.VMEM((2, ROWS, width), jnp.float32),
            pltpu.VMEM((2, 2, ROWS, BLK), jnp.float32),
            pltpu.VMEM((width, TILE), jnp.float32),
            pltpu.VMEM(keys.shape, jnp.bfloat16),
        ],
        compiler_params=call_params(),
        cost_estimate=pl.CostEstimate(flops=25 * 10**9, bytes_accessed=10**7, transcendentals=10**7),
        name="gradients",
    )(info, keys, *own, *sibling, mine, theirs)

EXPERTS = 256
ROUTE_SCALE = 2.5
Z_NEAR, Y_RING, CORES, X_RING, Z_FAR = 8, 4, 2, 4, 2
REACH = 4
GRID = ("z", "y", "core", "x", "far")


def around(value, axis, steps, count=4):
    return lax.ppermute(value, axis, [(i, (i + steps) % count) for i in range(count)])


def along_z(value, steps):
    pairs = [(i, i + steps) for i in range(Z_NEAR) if 0 <= i + steps < Z_NEAR]
    return lax.ppermute(value, "z", pairs)


def other_core(value):
    return around(value, "core", 1, CORES)


def after(value, event):
    return lax.optimization_barrier((value, event))[0]


def plus(*terms):
    return sum(t.astype(jnp.float32) for t in terms).astype(jnp.bfloat16)


def in_plane(value, stage, steps):
    pairs = []
    for place in np.ndindex(Z_NEAR, Y_RING, CORES, X_RING, Z_FAR):
        there = list(place)
        axis = 3 if place[2] == stage else 1
        there[axis] = (there[axis] + steps) % 4
        pairs.append(tuple(int(np.ravel_multi_index(p, (Z_NEAR, Y_RING, CORES, X_RING, Z_FAR))) for p in (place, there)))
    return lax.ppermute(value, GRID, pairs)


def gather_keys(latents, meanwhile):
    quarter = latents.shape[0] // X_RING
    piece = lax.dynamic_slice_in_dim(latents, lax.axis_index("x") * quarter, quarter, 0)
    planes = jnp.stack([along_z(piece, REACH - p) for p in range(REACH)] + [piece])
    planes = after(planes, meanwhile)
    line = jnp.stack([planes, in_plane(planes, 0, -1), in_plane(planes, 0, 2), in_plane(planes, 0, 1)])
    up, down = in_plane(line, 1, 1), in_plane(line, 1, -1)
    return [line, down, in_plane(up, 1, 1), up]


def reduce_in_plane(terms):
    far = plus(terms[1], in_plane(terms[2], 1, 1))
    line = plus(terms[0], in_plane(far, 1, 1), in_plane(terms[3], 1, -1))
    return plus(line[0], in_plane(line[1], 0, 1), in_plane(line[2], 0, 2), in_plane(line[3], 0, -1)), far


def reduce_along_z(planes):
    total = planes[REACH].astype(jnp.float32)
    for p in range(REACH):
        total = total + along_z(planes[p], p - REACH).astype(jnp.float32)
    return total


def with_start(rows, block_start):
    start = jnp.full((16, rows.shape[1]), block_start[0].astype(rows.dtype))
    return jnp.concatenate([rows, start])


def attention_info(block_start, sibling_start):
    z, y, core, x = (lax.axis_index(a) for a in ("z", "y", "core", "x"))
    starts = jnp.stack([block_start[0], sibling_start.astype(jnp.int32)]) - 2 * Y_RING * (z - REACH)
    lows = (starts - core + 1) // 2
    own = REACH * Y_RING + y
    return jnp.stack([lows[0], lows[1], own - core, own, y, x, core]).astype(jnp.int32)


def partner(value, bit):
    if bit == 0:
        return around(value, "far", 1, Z_FAR)
    return lax.ppermute(value, "x", [(i, (i ^ 1) if bit == 1 else 3 - i) for i in range(X_RING)])


def position(x, far):
    return (x ^ (x // 2)) * 2 + far


def gate_products(every, expert_out, me):
    saved = expert_out[0, 0]
    products = [jnp.einsum("scd,rtd->srct", saved, rows, preferred_element_type=jnp.float32) for rows in every]
    products = jnp.concatenate(products, axis=1)
    group = jnp.arange(X_RING * Z_FAR, dtype=jnp.int32)
    apart = position(group // Z_FAR, group % Z_FAR) ^ me
    same = apart[:, None] == group[None, :]
    terms = jnp.sum(jnp.where(same[:, :, None, None], products, 0.0), axis=0)
    return terms.reshape(X_RING, Z_FAR, -1)


def letter(rows, gates):
    high = gates.astype(jnp.bfloat16)
    rest = (gates - high.astype(jnp.float32)).astype(jnp.bfloat16)
    both = jnp.concatenate([high, rest])
    room = ((0, 16 - both.shape[0]), (0, rows.shape[1] - both.shape[1]))
    return jnp.concatenate([rows, jnp.pad(both, room)])


def opened(mail, count, size):
    both = mail[-16:, :size].astype(jnp.float32)
    return mail[:-16], both[:count] + both[count:2 * count]


def settle(part, gates, meanwhile):
    size = gates.shape[2]
    x = lax.axis_index("x")
    mail = around(letter(part.astype(jnp.bfloat16), gates[:, 1]), "far", 1, Z_FAR)
    rows, theirs = opened(mail, X_RING, size)
    whole = plus(part, after(rows, meanwhile))
    gates = jnp.stack([gates[:, 0], theirs], axis=1)
    even = x % 2 == 0
    ahead, behind = jnp.where(even, gates[1], gates[2]), jnp.where(even, gates[2], gates[1])
    mails = [
        around(letter(whole, behind), "x", -1),
        around(letter(whole, gates[3]), "x", 2),
        around(letter(whole, ahead), "x", 1),
    ]
    (r1, g1), (r2, g2), (r3, g3) = [opened(mail, Z_FAR, size) for mail in mails]
    twice = jnp.stack([whole, r1, r2, r3, whole, r1, r2, r3])
    block = lax.dynamic_slice_in_dim(twice, (X_RING - x) % X_RING, X_RING, 0)
    gates = jnp.stack([gates[0], jnp.where(even, g1, g3), jnp.where(even, g3, g1), g2])
    return block.reshape(-1, block.shape[2]), gates.reshape(X_RING * Z_FAR, size)


def logit_part(gates, affinity, expert_ids, me):
    tokens, top = expert_ids.shape
    groups, size = gates.shape
    owner = (expert_ids // (EXPERTS // groups)).reshape(-1)
    order = jnp.arange(tokens * top, dtype=jnp.int32)
    before = jnp.logical_and(owner[:, None] == owner[None, :], order[:, None] > order[None, :])
    slot = jnp.sum(before.astype(jnp.int32), axis=1)
    there = position(owner // Z_FAR, owner % Z_FAR) ^ me
    place = (there * size + slot * tokens + order // top).reshape(tokens, top)
    index = jnp.arange(groups * size, dtype=jnp.int32).reshape(groups, size)
    chosen = place[:, :, None, None] == index
    gate_grad = jnp.sum(jnp.where(chosen, gates, 0.0), axis=(2, 3))
    total = jnp.sum(affinity, axis=1, keepdims=True)
    weighted = jnp.sum(gate_grad * affinity, axis=1, keepdims=True) / total
    return ROUTE_SCALE / total * (gate_grad - weighted) * affinity * (1.0 - affinity)


def local(queries, latents, out_grad, block_start, moe_grad, affinity, expert_ids, expert_out):
    ours = prepare(queries, out_grad)
    kv = gather_keys(latents, ours)
    sibling_grad = other_core(with_start(out_grad, block_start))
    others = prepare(other_core(queries), sibling_grad)
    me = position(lax.axis_index("x"), lax.axis_index("far"))
    two = jnp.stack([moe_grad, partner(moe_grad, 0)])
    info = attention_info(block_start, sibling_grad[out_grad.shape[0], 0])
    four = jnp.concatenate([two, partner(after(two, kv[2]), 1)])
    mine, keys = stats(info, ours, others, kv)
    every = [four, partner(after(four, mine), 2)]
    own, sibling, *terms = gradients(info, keys, ours, others, mine, other_core(mine), [len(k) for k in kv])
    planes, middle = reduce_in_plane(terms)
    query_grad = plus(own, other_core(after(sibling, middle)))
    gates = gate_products(every, after(expert_out, middle), me)
    latent_grad, gates = settle(reduce_along_z(planes), gates, query_grad)
    return (query_grad, latent_grad, logit_part(gates, affinity, expert_ids, me))


def solution(mesh):
    parts = mesh.devices.reshape(Z_NEAR, Y_RING, CORES, X_RING, Z_FAR)
    grid = Mesh(parts, GRID)
    ctx, exp = GRID[:3], GRID[3:]
    in_specs = (
        P(ctx, exp),
        P(ctx, None),
        P(ctx, exp),
        P(ctx),
        P(ctx + exp, None),
        P(ctx + exp, None),
        P(ctx + exp, None),
        P(ctx, exp, None, None, None),
    )
    out_specs = (P(ctx, exp), P(ctx, None), P(ctx + exp, None))
    return jax.shard_map(local, mesh=grid, in_specs=in_specs, out_specs=out_specs, check_vma=False)
```

```python
import jax
import jax.numpy as jnp
import numpy as np
from jax import lax
from jax.experimental import pallas as pl
from jax.experimental.pallas import tpu as pltpu
from jax.sharding import Mesh, PartitionSpec as P

SCALE = 192.0 ** (-0.5)
EXP2_SCALE = SCALE * 1.4426950408889634
NEG = -1e30
BLK = 128
TILE = 2 * BLK
CHUNK = 512
ROWS = 8 * BLK
NT = (((1,), (1,)), ((), ()))
TN = (((0,), (0,)), ((), ()))


def piece_places(info, tile):
    places = []
    for half in range(2):
        block = 2 * tile + half
        plane, turn = block >> 2, (block + 4 - info[4]) & 3
        first = jnp.where(info[6] == 0, turn * 20, turn * 5) + plane
        step = jnp.where(info[6] == 0, 5, 20)
        places += [first + i * step for i in range(4)]
    return places


def tile_keys(info, keys, tile):
    return jnp.concatenate([keys[place] for place in piece_places(info, tile)], axis=0)


def tile_span(info):
    own = info[3]
    last = own // 2
    first = jnp.minimum(jnp.minimum(info[0], info[1]) // 2, last)
    return first, last


def row_limits(info, group):
    return (info[0], info[3]) if group == 0 else (info[1], info[2])


def block_bias(info, group, tile):
    low, high = row_limits(info, group)
    return [jnp.where(jnp.logical_and(2 * tile + half >= low, 2 * tile + half <= high), 0.0, NEG)
            for half in range(2)]


def tile_used(info, group, tile):
    low, high = row_limits(info, group)
    return jnp.logical_and(2 * tile + 1 >= low, jnp.logical_and(2 * tile <= high, low <= high))


def column_bias(info, group, tile):
    first, second = block_bias(info, group, tile)
    place = lax.broadcasted_iota(jnp.int32, (1, TILE), 1)
    return jnp.where(place < BLK, first, second)


def later_keys(info, tile, s, row_start):
    place = lax.broadcasted_iota(jnp.int32, s.shape, 1)
    row = (lax.broadcasted_iota(jnp.int32, s.shape, 0) + row_start) % BLK
    size = BLK // 4
    within = place % BLK
    key = (within // size + info[5]) % 4 * size + within % size
    own = 2 * tile + place // BLK == info[3]
    return jnp.where(jnp.logical_and(own, key > row), NEG, s)


def masked_columns(info, s, group, tile, diagonal):
    bias = block_bias(info, group, tile)
    halves = []
    for half in range(2):
        part = s[half * BLK:(half + 1) * BLK] + bias[half]
        if diagonal:
            place = lax.broadcasted_iota(jnp.int32, part.shape, 0)
            row = lax.broadcasted_iota(jnp.int32, part.shape, 1) % BLK
            size = BLK // 4
            key = (place // size + info[5]) % 4 * size + place % size
            later = jnp.logical_and(key > row, info[3] == 2 * tile + half)
            part = jnp.where(later, NEG, part)
        halves.append(part)
    return halves[0], halves[1]


def split_heads(rows, heads):
    width = heads.shape[1]
    for pair in range(ROWS // BLK // 2):
        both = rows[:BLK, 2 * width * pair:2 * width * (pair + 1)]
        heads[pl.ds(2 * pair * BLK, BLK), :] = both[:, :width]
        heads[pl.ds((2 * pair + 1) * BLK, BLK), :] = both[:, width:]


def join_heads(heads, rows):
    width = heads.shape[1]
    for pair in range(ROWS // BLK // 2):
        both = [heads[pl.ds((2 * pair + i) * BLK, BLK), :] * SCALE for i in range(2)]
        rows[:, 2 * width * pair:2 * width * (pair + 1)] = jnp.concatenate(both, axis=1).astype(rows.dtype)


def prepare_kernel(q, g, qs, gs, qt, gt):
    split_heads(q, qs)
    split_heads(g, gs)
    for h in range(ROWS // BLK):
        rs = pl.ds(h * BLK, BLK)
        qt[:, h * BLK:(h + 1) * BLK] = qs[rs, :].T
        gt[:, h * BLK:(h + 1) * BLK] = gs[rs, :].T


def stats_kernel(info, q_own, g_own, q_sib, g_sib, *refs):
    *kv, out, keys, m_ref, l_ref, d_ref = refs
    width, lat = q_own.shape[1], g_own.shape[1]
    begin = 0
    for pieces in kv:
        count = pieces.shape[0] * pieces.shape[1]
        keys[pl.ds(begin, count)] = pieces[...].reshape((count,) + pieces.shape[2:])
        begin += count
    m_ref[...] = jnp.full_like(m_ref, NEG)
    l_ref[...] = jnp.zeros_like(l_ref)
    d_ref[...] = jnp.zeros_like(d_ref)

    def visit(tile, group, q, g, diagonal):
        k = tile_keys(info, keys, tile)
        for r in range(ROWS // CHUNK):
            rs = pl.ds(r * CHUNK, CHUNK)
            s = lax.dot_general(k, q[rs, :], NT, preferred_element_type=jnp.float32)
            dp = lax.dot_general(k[:, :lat], g[rs, :], NT, preferred_element_type=jnp.float32)
            s = jnp.concatenate(masked_columns(info, s, group, tile, diagonal), axis=0)
            s = s.reshape(TILE // 8, 8, CHUNK)
            dp = dp.reshape(TILE // 8, 8, CHUNK)
            before = m_ref[group, :, rs]
            top = jnp.maximum(before, jnp.max(s, axis=0))
            shrink = jnp.exp2((before - top) * EXP2_SCALE)
            p = jnp.exp2((s - top[None]) * EXP2_SCALE)
            m_ref[group, :, rs] = top
            l_ref[group, :, rs] = l_ref[group, :, rs] * shrink + jnp.sum(p, axis=0)
            d_ref[group, :, rs] = d_ref[group, :, rs] * shrink + jnp.sum(p * dp, axis=0)

    def step(tile, diagonal):
        for group, (q, g) in enumerate(((q_own, g_own), (q_sib, g_sib))):
            @pl.when(tile_used(info, group, tile))
            def _(group=group, q=q, g=g):
                visit(tile, group, q, g, diagonal and group == 0)

    first, last = tile_span(info)

    def body(tile, _):
        step(tile, False)
        return 0

    lax.fori_loop(first, last, body, 0)
    step(last, True)

    for group in range(2):
        m, l, d = m_ref[group], l_ref[group], d_ref[group]
        top = jnp.max(m, axis=0, keepdims=True)
        weight = jnp.exp2((m - top) * EXP2_SCALE)
        out[group, 0:1, :] = top
        out[group, 1:2, :] = jnp.sum(l * weight, axis=0, keepdims=True)
        out[group, 2:3, :] = jnp.sum(d * weight, axis=0, keepdims=True)
        out[group, 3:8, :] = jnp.zeros((5, ROWS), jnp.float32)


def grad_kernel(info, keys, *refs):
    rows, (mine, theirs, dq_own, dq_sib) = (refs[:4], refs[4:8]), refs[8:12]
    *terms, acc, norm, total, sums = refs[12:]
    width, lat = rows[0][0].shape[1], rows[0][1].shape[1]
    first, last = tile_span(info)
    sums[...] = jnp.zeros_like(sums)
    acc[...] = jnp.zeros_like(acc)

    for group in range(2):
        a, b = mine[group], theirs[1 - group]
        top = jnp.maximum(a[0:1], b[0:1])
        wa = jnp.exp2((a[0:1] - top) * EXP2_SCALE)
        wb = jnp.exp2((b[0:1] - top) * EXP2_SCALE)
        whole = a[1:2] * wa + b[1:2] * wb
        level = top * EXP2_SCALE + jnp.log2(whole)
        delta = (a[2:3] * wa + b[2:3] * wb) / whole
        for h in range(ROWS // BLK):
            cs = slice(h * BLK, (h + 1) * BLK)
            rs = pl.ds(h * BLK, BLK)
            norm[0, group, rs, :] = jnp.broadcast_to(level[:, cs], (BLK, BLK)).T
            norm[1, group, rs, :] = jnp.broadcast_to(delta[:, cs], (BLK, BLK)).T

    def visit(tile, group, diagonal):
        qs, gs, qt, gt = rows[group]
        k = tile_keys(info, keys, tile)
        bias = column_bias(info, group, tile)
        p_all, ds_all = [], []
        for r in range(ROWS // CHUNK):
            rs = pl.ds(r * CHUNK, CHUNK)
            s = lax.dot_general(qs[rs, :], k, NT, preferred_element_type=jnp.float32) + bias
            dp = lax.dot_general(gs[rs, :], k[:, :lat], NT, preferred_element_type=jnp.float32)
            if diagonal:
                s = later_keys(info, tile, s, r * CHUNK)
            level, delta = norm[0, group, rs, :], norm[1, group, rs, :]
            p, ds = [], []
            for h in range(2):
                cs = slice(h * BLK, (h + 1) * BLK)
                prob = jnp.exp2(s[:, cs] * EXP2_SCALE - level)
                ds.append((prob * (dp[:, cs] - delta)).astype(jnp.bfloat16))
                p.append(prob.astype(jnp.bfloat16))
            ds = jnp.concatenate(ds, axis=1)
            acc[group, rs, :] += jnp.dot(ds, k, preferred_element_type=jnp.float32)
            p_all.append(jnp.concatenate(p, axis=1))
            ds_all.append(ds)
        ds, p = jnp.concatenate(ds_all, axis=0), jnp.concatenate(p_all, axis=0)
        dk = jnp.dot(qt[...], ds, preferred_element_type=jnp.float32) * SCALE
        dv = jnp.dot(gt[...], p, preferred_element_type=jnp.float32)
        total[:lat, :] += dk[:lat] + dv
        total[lat:, :] += dk[lat:]

    def step(tile, diagonal):
        total[...] = jnp.zeros_like(total)
        for group in range(2):
            @pl.when(tile_used(info, group, tile))
            def _(group=group):
                visit(tile, group, diagonal and group == 0)
        pieces = total[...].T.astype(jnp.bfloat16).reshape((8, -1, width))
        for i, place in enumerate(piece_places(info, tile)):
            sums[place] = pieces[i]

    def body(tile, _):
        step(tile, False)
        return 0

    lax.fori_loop(first, last, body, 0)
    step(last, True)
    join_heads(acc.at[0], dq_own)
    join_heads(acc.at[1], dq_sib)

    begin = 0
    for pieces in terms:
        count = pieces.shape[0] * pieces.shape[1]
        pieces[...] = sums[pl.ds(begin, count)].reshape(pieces.shape)
        begin += count


def call_params():
    return pltpu.CompilerParams(vmem_limit_bytes=18 * 2**20)


def vmem(count):
    return [pl.BlockSpec(memory_space=pltpu.VMEM)] * count


def shaped(*shape, kind=jnp.bfloat16):
    return jax.ShapeDtypeStruct(shape, kind)


def prepare(q, g):
    heads = ROWS // BLK
    width, lat = q.shape[1] // heads, g.shape[1] // heads
    return pl.pallas_call(
        prepare_kernel,
        out_shape=[shaped(ROWS, width), shaped(ROWS, lat), shaped(width, ROWS), shaped(lat, ROWS)],
        in_specs=vmem(2),
        out_specs=vmem(4),
        compiler_params=call_params(),
        name="prepare",
    )(q, g)


def stats(info, own, sibling, kv):
    planes, piece, width = kv[0].shape[1:]
    return pl.pallas_call(
        stats_kernel,
        out_shape=[shaped(2, 8, ROWS, kind=jnp.float32), shaped(16 * planes, piece, width)],
        in_specs=[pl.BlockSpec(memory_space=pltpu.SMEM)] + vmem(4 + len(kv)),
        out_specs=vmem(2),
        scratch_shapes=[pltpu.VMEM((2, 8, ROWS), jnp.float32)] * 3,
        compiler_params=call_params(),
        cost_estimate=pl.CostEstimate(flops=10 * 10**9, bytes_accessed=10**7, transcendentals=10**7),
        name="stats",
    )(info, *own[:2], *sibling[:2], *kv)


def gradients(info, keys, own, sibling, mine, theirs, counts):
    width = own[0].shape[1]
    planes, piece = keys.shape[0] // 16, keys.shape[1]
    return pl.pallas_call(
        grad_kernel,
        out_shape=[shaped(BLK, ROWS // BLK * width)] * 2 + [shaped(n, planes, piece, width) for n in counts],
        in_specs=[pl.BlockSpec(memory_space=pltpu.SMEM)] + vmem(11),
        out_specs=vmem(2 + len(counts)),
        scratch_shapes=[
            pltpu.VMEM((2, ROWS, width), jnp.float32),
            pltpu.VMEM((2, 2, ROWS, BLK), jnp.float32),
            pltpu.VMEM((width, TILE), jnp.float32),
            pltpu.VMEM(keys.shape, jnp.bfloat16),
        ],
        compiler_params=call_params(),
        cost_estimate=pl.CostEstimate(flops=25 * 10**9, bytes_accessed=10**7, transcendentals=10**7),
        name="gradients",
    )(info, keys, *own, *sibling, mine, theirs)

EXPERTS = 256
ROUTE_SCALE = 2.5
Z_NEAR, Y_RING, CORES, X_RING, Z_FAR = 8, 4, 2, 4, 2
REACH = 4
GRID = ("z", "y", "core", "x", "far")


def around(value, axis, steps, count=4):
    return lax.ppermute(value, axis, [(i, (i + steps) % count) for i in range(count)])


def along_z(value, steps):
    pairs = [(i, i + steps) for i in range(Z_NEAR) if 0 <= i + steps < Z_NEAR]
    return lax.ppermute(value, "z", pairs)


def other_core(value):
    return around(value, "core", 1, CORES)


def after(value, event):
    return lax.optimization_barrier((value, event))[0]


def plus(*terms):
    return sum(t.astype(jnp.float32) for t in terms).astype(jnp.bfloat16)


def in_plane(value, stage, steps):
    pairs = []
    for place in np.ndindex(Z_NEAR, Y_RING, CORES, X_RING, Z_FAR):
        there = list(place)
        axis = 3 if place[2] == stage else 1
        there[axis] = (there[axis] + steps) % 4
        pairs.append(tuple(int(np.ravel_multi_index(p, (Z_NEAR, Y_RING, CORES, X_RING, Z_FAR))) for p in (place, there)))
    return lax.ppermute(value, GRID, pairs)


def gather_keys(latents, meanwhile):
    quarter = latents.shape[0] // X_RING
    piece = lax.dynamic_slice_in_dim(latents, lax.axis_index("x") * quarter, quarter, 0)
    planes = jnp.stack([along_z(piece, REACH - p) for p in range(REACH)] + [piece])
    planes = after(planes, meanwhile)
    line = jnp.stack([planes, in_plane(planes, 0, -1), in_plane(planes, 0, 2), in_plane(planes, 0, 1)])
    up, down = in_plane(line, 1, 1), in_plane(line, 1, -1)
    return [line, down, in_plane(line, 1, 2), up]


def reduce_in_plane(terms):
    far = in_plane(terms[3], 1, -1)
    line = plus(terms[0], in_plane(terms[1], 1, 1), in_plane(terms[2], 1, 2), far)
    return plus(line[0], in_plane(line[1], 0, 1), in_plane(line[2], 0, 2), in_plane(line[3], 0, -1)), far


def reduce_along_z(planes):
    total = planes[REACH].astype(jnp.float32)
    for p in range(REACH):
        total = total + along_z(planes[p], p - REACH).astype(jnp.float32)
    return total


def with_start(rows, block_start):
    start = jnp.full((16, rows.shape[1]), block_start[0].astype(rows.dtype))
    return jnp.concatenate([rows, start])


def attention_info(block_start, sibling_start):
    z, y, core, x = (lax.axis_index(a) for a in ("z", "y", "core", "x"))
    starts = jnp.stack([block_start[0], sibling_start.astype(jnp.int32)]) - 2 * Y_RING * (z - REACH)
    lows = (starts - core + 1) // 2
    own = REACH * Y_RING + y
    return jnp.stack([lows[0], lows[1], own - core, own, y, x, core]).astype(jnp.int32)


def partner(value, bit):
    if bit == 0:
        return around(value, "far", 1, Z_FAR)
    return lax.ppermute(value, "x", [(i, (i ^ 1) if bit == 1 else 3 - i) for i in range(X_RING)])


def position(x, far):
    return (x ^ (x // 2)) * 2 + far


def gate_products(every, expert_out, me):
    saved = expert_out[0, 0]
    products = [jnp.einsum("scd,rtd->srct", saved, rows, preferred_element_type=jnp.float32) for rows in every]
    products = jnp.concatenate(products, axis=1)
    group = jnp.arange(X_RING * Z_FAR, dtype=jnp.int32)
    apart = position(group // Z_FAR, group % Z_FAR) ^ me
    same = apart[:, None] == group[None, :]
    terms = jnp.sum(jnp.where(same[:, :, None, None], products, 0.0), axis=0)
    return terms.reshape(X_RING, Z_FAR, -1)


def letter(rows, gates):
    high = gates.astype(jnp.bfloat16)
    rest = (gates - high.astype(jnp.float32)).astype(jnp.bfloat16)
    both = jnp.concatenate([high, rest])
    room = ((0, 16 - both.shape[0]), (0, rows.shape[1] - both.shape[1]))
    return jnp.concatenate([rows, jnp.pad(both, room)])


def opened(mail, count, size):
    both = mail[-16:, :size].astype(jnp.float32)
    return mail[:-16], both[:count] + both[count:2 * count]


def settle(part, gates, meanwhile):
    size = gates.shape[2]
    x = lax.axis_index("x")
    mail = around(letter(part.astype(jnp.bfloat16), gates[:, 1]), "far", 1, Z_FAR)
    rows, theirs = opened(mail, X_RING, size)
    whole = plus(part, after(rows, meanwhile))
    gates = jnp.stack([gates[:, 0], theirs], axis=1)
    even = x % 2 == 0
    ahead, behind = jnp.where(even, gates[1], gates[2]), jnp.where(even, gates[2], gates[1])
    mails = [
        around(letter(whole, behind), "x", -1),
        around(letter(whole, gates[3]), "x", 2),
        around(letter(whole, ahead), "x", 1),
    ]
    (r1, g1), (r2, g2), (r3, g3) = [opened(mail, Z_FAR, size) for mail in mails]
    twice = jnp.stack([whole, r1, r2, r3, whole, r1, r2, r3])
    block = lax.dynamic_slice_in_dim(twice, (X_RING - x) % X_RING, X_RING, 0)
    gates = jnp.stack([gates[0], jnp.where(even, g1, g3), jnp.where(even, g3, g1), g2])
    return block.reshape(-1, block.shape[2]), gates.reshape(X_RING * Z_FAR, size)


def logit_part(gates, affinity, expert_ids, me):
    tokens, top = expert_ids.shape
    groups, size = gates.shape
    owner = (expert_ids // (EXPERTS // groups)).reshape(-1)
    order = jnp.arange(tokens * top, dtype=jnp.int32)
    before = jnp.logical_and(owner[:, None] == owner[None, :], order[:, None] > order[None, :])
    slot = jnp.sum(before.astype(jnp.int32), axis=1)
    there = position(owner // Z_FAR, owner % Z_FAR) ^ me
    place = (there * size + slot * tokens + order // top).reshape(tokens, top)
    index = jnp.arange(groups * size, dtype=jnp.int32).reshape(groups, size)
    chosen = place[:, :, None, None] == index
    gate_grad = jnp.sum(jnp.where(chosen, gates, 0.0), axis=(2, 3))
    total = jnp.sum(affinity, axis=1, keepdims=True)
    weighted = jnp.sum(gate_grad * affinity, axis=1, keepdims=True) / total
    return ROUTE_SCALE / total * (gate_grad - weighted) * affinity * (1.0 - affinity)


def local(queries, latents, out_grad, block_start, moe_grad, affinity, expert_ids, expert_out):
    ours = prepare(queries, out_grad)
    kv = gather_keys(latents, ours)
    sibling_grad = other_core(with_start(out_grad, block_start))
    others = prepare(other_core(queries), sibling_grad)
    me = position(lax.axis_index("x"), lax.axis_index("far"))
    two = jnp.stack([moe_grad, partner(moe_grad, 0)])
    info = attention_info(block_start, sibling_grad[out_grad.shape[0], 0])
    four = jnp.concatenate([two, partner(after(two, kv[2]), 1)])
    mine, keys = stats(info, ours, others, kv)
    every = [four, partner(after(four, mine), 2)]
    own, sibling, *terms = gradients(info, keys, ours, others, mine, other_core(mine), [len(k) for k in kv])
    planes, middle = reduce_in_plane(terms)
    query_grad = plus(own, other_core(after(sibling, middle)))
    gates = gate_products(every, after(expert_out, middle), me)
    latent_grad, gates = settle(reduce_along_z(planes), gates, query_grad)
    return (query_grad, latent_grad, logit_part(gates, affinity, expert_ids, me))


def solution(mesh):
    parts = mesh.devices.reshape(Z_NEAR, Y_RING, CORES, X_RING, Z_FAR)
    grid = Mesh(parts, GRID)
    ctx, exp = GRID[:3], GRID[3:]
    in_specs = (
        P(ctx, exp),
        P(ctx, None),
        P(ctx, exp),
        P(ctx),
        P(ctx + exp, None),
        P(ctx + exp, None),
        P(ctx + exp, None),
        P(ctx, exp, None, None, None),
    )
    out_specs = (P(ctx, exp), P(ctx, None), P(ctx + exp, None))
    return jax.shard_map(local, mesh=grid, in_specs=in_specs, out_specs=out_specs, check_vma=False)
```

```python
import jax
import jax.numpy as jnp
import numpy as np
from jax import lax
from jax.experimental import pallas as pl
from jax.experimental.pallas import tpu as pltpu
from jax.sharding import Mesh, PartitionSpec as P

SCALE = 192.0 ** (-0.5)
EXP2_SCALE = SCALE * 1.4426950408889634
NEG = -1e30
BLK = 128
TILE = 2 * BLK
CHUNK = 512
ROWS = 8 * BLK
NT = (((1,), (1,)), ((), ()))
TN = (((0,), (0,)), ((), ()))


def piece_places(info, tile):
    places = []
    for half in range(2):
        block = 2 * tile + half
        plane, turn = block >> 2, (block + 4 - info[4]) & 3
        first = jnp.where(info[6] == 0, turn * 20, turn * 5) + plane
        step = jnp.where(info[6] == 0, 5, 20)
        places += [first + i * step for i in range(4)]
    return places


def tile_keys(info, keys, tile):
    return jnp.concatenate([keys[place] for place in piece_places(info, tile)], axis=0)


def tile_span(info):
    own = info[3]
    last = own // 2
    first = jnp.minimum(jnp.minimum(info[0], info[1]) // 2, last)
    return first, last


def row_limits(info, group):
    return (info[0], info[3]) if group == 0 else (info[1], info[2])


def block_bias(info, group, tile):
    low, high = row_limits(info, group)
    return [jnp.where(jnp.logical_and(2 * tile + half >= low, 2 * tile + half <= high), 0.0, NEG)
            for half in range(2)]


def tile_used(info, group, tile):
    low, high = row_limits(info, group)
    return jnp.logical_and(2 * tile + 1 >= low, jnp.logical_and(2 * tile <= high, low <= high))


def column_bias(info, group, tile):
    first, second = block_bias(info, group, tile)
    place = lax.broadcasted_iota(jnp.int32, (1, TILE), 1)
    return jnp.where(place < BLK, first, second)


def later_keys(info, tile, s, row_start):
    place = lax.broadcasted_iota(jnp.int32, s.shape, 1)
    row = (lax.broadcasted_iota(jnp.int32, s.shape, 0) + row_start) % BLK
    size = BLK // 4
    within = place % BLK
    key = (within // size + info[5]) % 4 * size + within % size
    own = 2 * tile + place // BLK == info[3]
    return jnp.where(jnp.logical_and(own, key > row), NEG, s)


def masked_columns(info, s, group, tile, diagonal):
    bias = block_bias(info, group, tile)
    halves = []
    for half in range(2):
        part = s[half * BLK:(half + 1) * BLK] + bias[half]
        if diagonal:
            place = lax.broadcasted_iota(jnp.int32, part.shape, 0)
            row = lax.broadcasted_iota(jnp.int32, part.shape, 1) % BLK
            size = BLK // 4
            key = (place // size + info[5]) % 4 * size + place % size
            later = jnp.logical_and(key > row, info[3] == 2 * tile + half)
            part = jnp.where(later, NEG, part)
        halves.append(part)
    return halves[0], halves[1]


def split_heads(rows, heads):
    width = heads.shape[1]
    for pair in range(ROWS // BLK // 2):
        both = rows[:BLK, 2 * width * pair:2 * width * (pair + 1)]
        heads[pl.ds(2 * pair * BLK, BLK), :] = both[:, :width]
        heads[pl.ds((2 * pair + 1) * BLK, BLK), :] = both[:, width:]


def join_heads(heads, rows):
    width = heads.shape[1]
    for pair in range(ROWS // BLK // 2):
        both = [heads[pl.ds((2 * pair + i) * BLK, BLK), :] * SCALE for i in range(2)]
        rows[:, 2 * width * pair:2 * width * (pair + 1)] = jnp.concatenate(both, axis=1).astype(rows.dtype)


def prepare_kernel(q, g, qs, gs, qt, gt):
    split_heads(q, qs)
    split_heads(g, gs)
    for h in range(ROWS // BLK):
        rs = pl.ds(h * BLK, BLK)
        qt[:, h * BLK:(h + 1) * BLK] = qs[rs, :].T
        gt[:, h * BLK:(h + 1) * BLK] = gs[rs, :].T


def stats_kernel(info, q_own, g_own, q_sib, g_sib, *refs):
    *kv, out, keys, m_ref, l_ref, d_ref = refs
    width, lat = q_own.shape[1], g_own.shape[1]
    begin = 0
    for pieces in kv:
        count = pieces.shape[0] * pieces.shape[1]
        keys[pl.ds(begin, count)] = pieces[...].reshape((count,) + pieces.shape[2:])
        begin += count
    m_ref[...] = jnp.full_like(m_ref, NEG)
    l_ref[...] = jnp.zeros_like(l_ref)
    d_ref[...] = jnp.zeros_like(d_ref)

    def visit(tile, group, q, g, diagonal):
        k = tile_keys(info, keys, tile)
        for r in range(ROWS // CHUNK):
            rs = pl.ds(r * CHUNK, CHUNK)
            s = lax.dot_general(k, q[rs, :], NT, preferred_element_type=jnp.float32)
            dp = lax.dot_general(k[:, :lat], g[rs, :], NT, preferred_element_type=jnp.float32)
            s = jnp.concatenate(masked_columns(info, s, group, tile, diagonal), axis=0)
            s = s.reshape(TILE // 8, 8, CHUNK)
            dp = dp.reshape(TILE // 8, 8, CHUNK)
            before = m_ref[group, :, rs]
            top = jnp.maximum(before, jnp.max(s, axis=0))
            shrink = jnp.exp2((before - top) * EXP2_SCALE)
            p = jnp.exp2((s - top[None]) * EXP2_SCALE)
            m_ref[group, :, rs] = top
            l_ref[group, :, rs] = l_ref[group, :, rs] * shrink + jnp.sum(p, axis=0)
            d_ref[group, :, rs] = d_ref[group, :, rs] * shrink + jnp.sum(p * dp, axis=0)

    def step(tile, diagonal):
        for group, (q, g) in enumerate(((q_own, g_own), (q_sib, g_sib))):
            @pl.when(tile_used(info, group, tile))
            def _(group=group, q=q, g=g):
                visit(tile, group, q, g, diagonal and group == 0)

    first, last = tile_span(info)

    def body(tile, _):
        step(tile, False)
        return 0

    lax.fori_loop(first, last, body, 0)
    step(last, True)

    for group in range(2):
        m, l, d = m_ref[group], l_ref[group], d_ref[group]
        top = jnp.max(m, axis=0, keepdims=True)
        weight = jnp.exp2((m - top) * EXP2_SCALE)
        out[group, 0:1, :] = top
        out[group, 1:2, :] = jnp.sum(l * weight, axis=0, keepdims=True)
        out[group, 2:3, :] = jnp.sum(d * weight, axis=0, keepdims=True)
        out[group, 3:8, :] = jnp.zeros((5, ROWS), jnp.float32)


def grad_kernel(info, keys, *refs):
    rows, (mine, theirs, dq_own, dq_sib) = (refs[:4], refs[4:8]), refs[8:12]
    *terms, acc, norm, total, sums = refs[12:]
    width, lat = rows[0][0].shape[1], rows[0][1].shape[1]
    first, last = tile_span(info)
    sums[...] = jnp.zeros_like(sums)
    acc[...] = jnp.zeros_like(acc)

    for group in range(2):
        a, b = mine[group], theirs[1 - group]
        top = jnp.maximum(a[0:1], b[0:1])
        wa = jnp.exp2((a[0:1] - top) * EXP2_SCALE)
        wb = jnp.exp2((b[0:1] - top) * EXP2_SCALE)
        whole = a[1:2] * wa + b[1:2] * wb
        level = top * EXP2_SCALE + jnp.log2(whole)
        delta = (a[2:3] * wa + b[2:3] * wb) / whole
        for h in range(ROWS // BLK):
            cs = slice(h * BLK, (h + 1) * BLK)
            rs = pl.ds(h * BLK, BLK)
            norm[0, group, rs, :] = jnp.broadcast_to(level[:, cs], (BLK, BLK)).T
            norm[1, group, rs, :] = jnp.broadcast_to(delta[:, cs], (BLK, BLK)).T

    def visit(tile, group, diagonal):
        qs, gs, qt, gt = rows[group]
        k = tile_keys(info, keys, tile)
        bias = column_bias(info, group, tile)
        p_all, ds_all = [], []
        for r in range(ROWS // CHUNK):
            rs = pl.ds(r * CHUNK, CHUNK)
            s = lax.dot_general(qs[rs, :], k, NT, preferred_element_type=jnp.float32) + bias
            dp = lax.dot_general(gs[rs, :], k[:, :lat], NT, preferred_element_type=jnp.float32)
            if diagonal:
                s = later_keys(info, tile, s, r * CHUNK)
            level, delta = norm[0, group, rs, :], norm[1, group, rs, :]
            p, ds = [], []
            for h in range(2):
                cs = slice(h * BLK, (h + 1) * BLK)
                prob = jnp.exp2(s[:, cs] * EXP2_SCALE - level)
                ds.append((prob * (dp[:, cs] - delta)).astype(jnp.bfloat16))
                p.append(prob.astype(jnp.bfloat16))
            ds = jnp.concatenate(ds, axis=1)
            acc[group, rs, :] += jnp.dot(ds, k, preferred_element_type=jnp.float32)
            p_all.append(jnp.concatenate(p, axis=1))
            ds_all.append(ds)
        ds, p = jnp.concatenate(ds_all, axis=0), jnp.concatenate(p_all, axis=0)
        dk = jnp.dot(qt[...], ds, preferred_element_type=jnp.float32) * SCALE
        dv = jnp.dot(gt[...], p, preferred_element_type=jnp.float32)
        total[:lat, :] += dk[:lat] + dv
        total[lat:, :] += dk[lat:]

    def step(tile, diagonal):
        total[...] = jnp.zeros_like(total)
        for group in range(2):
            @pl.when(tile_used(info, group, tile))
            def _(group=group):
                visit(tile, group, diagonal and group == 0)
        pieces = total[...].T.astype(jnp.bfloat16).reshape((8, -1, width))
        for i, place in enumerate(piece_places(info, tile)):
            sums[place] = pieces[i]

    def body(tile, _):
        step(tile, False)
        return 0

    lax.fori_loop(first, last, body, 0)
    step(last, True)
    join_heads(acc.at[0], dq_own)
    join_heads(acc.at[1], dq_sib)

    begin = 0
    for pieces in terms:
        count = pieces.shape[0] * pieces.shape[1]
        pieces[...] = sums[pl.ds(begin, count)].reshape(pieces.shape)
        begin += count


def call_params():
    return pltpu.CompilerParams(vmem_limit_bytes=18 * 2**20)


def vmem(count):
    return [pl.BlockSpec(memory_space=pltpu.VMEM)] * count


def shaped(*shape, kind=jnp.bfloat16):
    return jax.ShapeDtypeStruct(shape, kind)


def prepare(q, g):
    heads = ROWS // BLK
    width, lat = q.shape[1] // heads, g.shape[1] // heads
    return pl.pallas_call(
        prepare_kernel,
        out_shape=[shaped(ROWS, width), shaped(ROWS, lat), shaped(width, ROWS), shaped(lat, ROWS)],
        in_specs=vmem(2),
        out_specs=vmem(4),
        compiler_params=call_params(),
        name="prepare",
    )(q, g)


def stats(info, own, sibling, kv):
    planes, piece, width = kv[0].shape[1:]
    return pl.pallas_call(
        stats_kernel,
        out_shape=[shaped(2, 8, ROWS, kind=jnp.float32), shaped(16 * planes, piece, width)],
        in_specs=[pl.BlockSpec(memory_space=pltpu.SMEM)] + vmem(4 + len(kv)),
        out_specs=vmem(2),
        scratch_shapes=[pltpu.VMEM((2, 8, ROWS), jnp.float32)] * 3,
        compiler_params=call_params(),
        cost_estimate=pl.CostEstimate(flops=10 * 10**9, bytes_accessed=10**7, transcendentals=10**7),
        name="stats",
    )(info, *own[:2], *sibling[:2], *kv)


def gradients(info, keys, own, sibling, mine, theirs, counts):
    width = own[0].shape[1]
    planes, piece = keys.shape[0] // 16, keys.shape[1]
    return pl.pallas_call(
        grad_kernel,
        out_shape=[shaped(BLK, ROWS // BLK * width)] * 2 + [shaped(n, planes, piece, width) for n in counts],
        in_specs=[pl.BlockSpec(memory_space=pltpu.SMEM)] + vmem(11),
        out_specs=vmem(2 + len(counts)),
        scratch_shapes=[
            pltpu.VMEM((2, ROWS, width), jnp.float32),
            pltpu.VMEM((2, 2, ROWS, BLK), jnp.float32),
            pltpu.VMEM((width, TILE), jnp.float32),
            pltpu.VMEM(keys.shape, jnp.bfloat16),
        ],
        compiler_params=call_params(),
        cost_estimate=pl.CostEstimate(flops=25 * 10**9, bytes_accessed=10**7, transcendentals=10**7),
        name="gradients",
    )(info, keys, *own, *sibling, mine, theirs)

EXPERTS = 256
ROUTE_SCALE = 2.5
Z_NEAR, Y_RING, CORES, X_RING, Z_FAR = 8, 4, 2, 4, 2
REACH = 4
GRID = ("z", "y", "core", "x", "far")


def around(value, axis, steps, count=4):
    return lax.ppermute(value, axis, [(i, (i + steps) % count) for i in range(count)])


def along_z(value, steps):
    pairs = [(i, i + steps) for i in range(Z_NEAR) if 0 <= i + steps < Z_NEAR]
    return lax.ppermute(value, "z", pairs)


def other_core(value):
    return around(value, "core", 1, CORES)


def after(value, event):
    return lax.optimization_barrier((value, event))[0]


def plus(*terms):
    return sum(t.astype(jnp.float32) for t in terms).astype(jnp.bfloat16)


def in_plane(value, stage, steps):
    pairs = []
    for place in np.ndindex(Z_NEAR, Y_RING, CORES, X_RING, Z_FAR):
        there = list(place)
        axis = 3 if place[2] == stage else 1
        there[axis] = (there[axis] + steps) % 4
        pairs.append(tuple(int(np.ravel_multi_index(p, (Z_NEAR, Y_RING, CORES, X_RING, Z_FAR))) for p in (place, there)))
    return lax.ppermute(value, GRID, pairs)


def gather_keys(latents, meanwhile):
    quarter = latents.shape[0] // X_RING
    piece = lax.dynamic_slice_in_dim(latents, lax.axis_index("x") * quarter, quarter, 0)
    planes = jnp.stack([along_z(piece, REACH - p) for p in range(REACH)] + [piece])
    planes = after(planes, meanwhile)
    line = jnp.stack([planes, in_plane(planes, 0, -1), in_plane(planes, 0, 2), in_plane(planes, 0, 1)])
    up, down = in_plane(line, 1, 1), in_plane(line, 1, -1)
    return [line, down, in_plane(line, 1, 2), up]


def reduce_in_plane(terms):
    far = in_plane(terms[3], 1, -1)
    line = plus(terms[0], in_plane(terms[1], 1, 1), in_plane(terms[2], 1, 2), far)
    return plus(line[0], in_plane(line[1], 0, 1), in_plane(line[2], 0, 2), in_plane(line[3], 0, -1)), far


def reduce_along_z(planes):
    total = planes[REACH].astype(jnp.float32)
    for p in range(REACH):
        total = total + along_z(planes[p], p - REACH).astype(jnp.float32)
    return total


def with_start(rows, block_start):
    start = jnp.full((16, rows.shape[1]), block_start[0].astype(rows.dtype))
    return jnp.concatenate([rows, start])


def attention_info(block_start, sibling_start):
    z, y, core, x = (lax.axis_index(a) for a in ("z", "y", "core", "x"))
    starts = jnp.stack([block_start[0], sibling_start.astype(jnp.int32)]) - 2 * Y_RING * (z - REACH)
    lows = (starts - core + 1) // 2
    own = REACH * Y_RING + y
    return jnp.stack([lows[0], lows[1], own - core, own, y, x, core]).astype(jnp.int32)


def partner(value, bit):
    if bit == 0:
        return around(value, "far", 1, Z_FAR)
    return lax.ppermute(value, "x", [(i, (i ^ 1) if bit == 1 else 3 - i) for i in range(X_RING)])


def position(x, far):
    return (x ^ (x // 2)) * 2 + far


def gate_products(every, expert_out, me):
    saved = expert_out[0, 0]
    products = [jnp.einsum("scd,rtd->srct", saved, rows, preferred_element_type=jnp.float32) for rows in every]
    products = jnp.concatenate(products, axis=1)
    group = jnp.arange(X_RING * Z_FAR, dtype=jnp.int32)
    apart = position(group // Z_FAR, group % Z_FAR) ^ me
    label = group.reshape(2, 2, 2).swapaxes(1, 2).reshape(-1)
    same = apart[:, None] == label[None, :]
    terms = jnp.sum(jnp.where(same[:, :, None, None], products, 0.0), axis=0)
    return terms.reshape(2, 2, 2, -1).swapaxes(1, 2).reshape(X_RING, Z_FAR, -1)


def letter(rows, gates):
    high = gates.astype(jnp.bfloat16)
    rest = (gates - high.astype(jnp.float32)).astype(jnp.bfloat16)
    both = jnp.concatenate([high, rest])
    room = ((0, 16 - both.shape[0]), (0, rows.shape[1] - both.shape[1]))
    return jnp.concatenate([rows, jnp.pad(both, room)])


def opened(mail, count, size):
    both = mail[-16:, :size].astype(jnp.float32)
    return mail[:-16], both[:count] + both[count:2 * count]


def settle(part, gates, meanwhile):
    size = gates.shape[2]
    x = lax.axis_index("x")
    mail = around(letter(part.astype(jnp.bfloat16), gates[:, 1]), "far", 1, Z_FAR)
    rows, theirs = opened(mail, X_RING, size)
    whole = plus(part, after(rows, meanwhile))
    gates = jnp.stack([gates[:, 0], theirs], axis=1)
    even = x % 2 == 0
    ahead, behind = jnp.where(even, gates[1], gates[2]), jnp.where(even, gates[2], gates[1])
    mails = [
        around(letter(whole, behind), "x", -1),
        around(letter(whole, gates[3]), "x", 2),
        around(letter(whole, ahead), "x", 1),
    ]
    (r1, g1), (r2, g2), (r3, g3) = [opened(mail, Z_FAR, size) for mail in mails]
    twice = jnp.stack([whole, r1, r2, r3, whole, r1, r2, r3])
    block = lax.dynamic_slice_in_dim(twice, (X_RING - x) % X_RING, X_RING, 0)
    gates = jnp.stack([gates[0], jnp.where(even, g1, g3), jnp.where(even, g3, g1), g2])
    return block.reshape(-1, block.shape[2]), gates.reshape(X_RING * Z_FAR, size)


def logit_part(gates, affinity, expert_ids, me):
    tokens, top = expert_ids.shape
    groups, size = gates.shape
    owner = (expert_ids // (EXPERTS // groups)).reshape(-1)
    order = jnp.arange(tokens * top, dtype=jnp.int32)
    before = jnp.logical_and(owner[:, None] == owner[None, :], order[:, None] > order[None, :])
    slot = jnp.sum(before.astype(jnp.int32), axis=1)
    there = position(owner // Z_FAR, owner % Z_FAR) ^ me
    place = (there * size + slot * tokens + order // top).reshape(tokens, top)
    index = jnp.arange(groups * size, dtype=jnp.int32).reshape(groups, size)
    chosen = place[:, :, None, None] == index
    gate_grad = jnp.sum(jnp.where(chosen, gates, 0.0), axis=(2, 3))
    total = jnp.sum(affinity, axis=1, keepdims=True)
    weighted = jnp.sum(gate_grad * affinity, axis=1, keepdims=True) / total
    return ROUTE_SCALE / total * (gate_grad - weighted) * affinity * (1.0 - affinity)


def local(queries, latents, out_grad, block_start, moe_grad, affinity, expert_ids, expert_out):
    ours = prepare(queries, out_grad)
    kv = gather_keys(latents, ours)
    sibling_grad = other_core(with_start(out_grad, block_start))
    others = prepare(other_core(queries), sibling_grad)
    me = position(lax.axis_index("x"), lax.axis_index("far"))
    two = jnp.stack([moe_grad, partner(moe_grad, 1)])
    info = attention_info(block_start, sibling_grad[out_grad.shape[0], 0])
    four = jnp.concatenate([two, partner(two, 0)])
    mine, keys = stats(info, ours, others, kv)
    every = [four, partner(after(four, mine), 2)]
    own, sibling, *terms = gradients(info, keys, ours, others, mine, other_core(mine), [len(k) for k in kv])
    planes, middle = reduce_in_plane(terms)
    query_grad = plus(own, other_core(after(sibling, middle)))
    gates = gate_products(every, after(expert_out, middle), me)
    latent_grad, gates = settle(reduce_along_z(planes), gates, query_grad)
    return (query_grad, latent_grad, logit_part(gates, affinity, expert_ids, me))


def solution(mesh):
    parts = mesh.devices.reshape(Z_NEAR, Y_RING, CORES, X_RING, Z_FAR)
    grid = Mesh(parts, GRID)
    ctx, exp = GRID[:3], GRID[3:]
    in_specs = (
        P(ctx, exp),
        P(ctx, None),
        P(ctx, exp),
        P(ctx),
        P(ctx + exp, None),
        P(ctx + exp, None),
        P(ctx + exp, None),
        P(ctx, exp, None, None, None),
    )
    out_specs = (P(ctx, exp), P(ctx, None), P(ctx + exp, None))
    return jax.shard_map(local, mesh=grid, in_specs=in_specs, out_specs=out_specs, check_vma=False)
```
